512 devices in a mesh: wide: 64 (over y, z_hi, x, core), narrow: 8 (over z_lo).
Axes of the slice: x: 4, y: 4, z: 16 (z_hi: 2, z_lo: 8; z = z_hi * 8 + z_lo), core: 2. Of those that a mesh axis runs over, the one named last changes fastest.
Arguments:
- spectra: bfloat16 [384, 2, 2, 4096], P('wide', None, None, 'narrow'), may hold values from -6 to 6
- dead_mask: int32 [384], P('wide'), may hold values 0 or 1
- seg_offsets: int32 [384, 2], P('wide'), may hold values from 0 to 32767
- src_index: int32 [256], replicated, may hold values from 0 to 383, as said below
Outputs:
- correlations: float32 [256, 384, 512], P('narrow', 'wide')
The draws below stay inside these ranges and needn't reach their ends.
Inputs may be any that keep to these rules, and one draw needn't show every extreme that they name: `src_index`: source j is one of the 6 channels j // 4 * 6 to j // 4 * 6 + 5; the 4 sources of one block are distinct; source 0 is channel 0 and source 256 - 4 is channel 384 - 1.
All inputs are finite; a program needn't handle non-finite values. No bound on the sum of `dead_mask` on one device may be relied on, other than what follows from the above.
Results may differ from the reference program's by a relative error of at most 0.0013.
Values may be sent and summed in bfloat16 or wider, within the bound.
No kernel may reach another device: no remote copies, remote signals or barrier semaphores. Data moves between devices by JAX's collectives and lax.ppermute only.
A program may use at most 128 MiB of HBM per device.

```python
import math
import jax
import jax.numpy as jnp
from jax import lax

CH_DEV = 6
SEGS = 2
FREQS = 4096
NSAMP = 32768
LAGS = 512
SMOOTH = 64
SG = 4
SOURCES = 256
CHANNELS = 384


def block_choice(subkey, target):
    order = jax.random.permutation(subkey, CH_DEV).astype(jnp.int32)
    where_at = jnp.argmax(order == target).astype(jnp.int32)
    first = order[0]
    swapped = order.at[where_at].set(first).at[0].set(target)
    return jnp.where(target >= 0, swapped, order)[:SG]


def draw_src_index(key, part):
    key = jax.random.fold_in(key, 11)
    blocks = SOURCES // SG
    subkeys = jax.random.split(key, blocks)
    block_ids = jnp.arange(blocks, dtype=jnp.int32)
    targets = jnp.where(block_ids == 0, 0, jnp.where(block_ids == blocks - 1, CH_DEV - 1, -1)).astype(jnp.int32)
    chosen = jax.vmap(block_choice)(subkeys, targets).astype(jnp.int32)
    offset_rows = (block_ids * CH_DEV)[:, None]
    return (offset_rows + chosen).reshape(SOURCES)


def place_ends(drawn, rng, least, high):
    dims = drawn.shape
    place = [jax.random.randint(jax.random.fold_in(rng, axis), (), 0, dims[axis]) for axis in range(len(dims))]
    drawn = drawn.at[tuple(place)].set(least)
    longest = dims.index(max(dims))
    place[longest] = (place[longest] + 1) % dims[longest]
    return drawn.at[tuple(place)].set(high)


def block_scale(stream_key, dims, cuts, low, top_value):
    gain, own = 1.0, jax.random.fold_in(stream_key, 6)
    for axis_at, parts in cuts:
        steps = jnp.exp(jax.random.uniform(jax.random.fold_in(own, axis_at), (parts,), jnp.float32, low / len(cuts), top_value / len(cuts)))
        gain = gain * jnp.repeat(steps, dims[axis_at] // parts).reshape([-1 if axis == axis_at else 1 for axis in range(len(dims))])
    return gain


def normal_values(key, extent, scale, bound, shards=(), held_as=jnp.bfloat16):
    entries = scale * jax.random.normal(key, extent, jnp.float32)
    if shards:
        entries = entries * block_scale(key, extent, shards, -0.22, 0.18)
    return jnp.clip(entries, -bound, bound).astype(held_as)


def setup_inputs(seed: int = 0) -> dict:
    keys = jax.random.split(jax.random.key(seed), 5)
    spectra = normal_values(keys[0], (CHANNELS, SEGS, 2, FREQS), 1.0, 6.0, ((0, 64), (3, 8)))
    dead_mask = place_ends((jax.random.randint(keys[1], (CHANNELS,), 0, 8) < 7).astype(jnp.int32), jax.random.fold_in(keys[1], 1), 0, 1)
    seg_offsets = place_ends(jax.random.randint(keys[2], (CHANNELS, SEGS), 0, NSAMP), jax.random.fold_in(keys[2], 1), 0, NSAMP - 1).astype(jnp.int32)
    src_index = draw_src_index(jax.random.fold_in(keys[4], 71), 0)
    return {"spectra": spectra, "dead_mask": dead_mask, "seg_offsets": seg_offsets, "src_index": src_index}


EPSILON = 1e-06

def lag_table(first, length, lag_count):
    bins = first + jnp.arange(length, dtype=jnp.int32) + 1
    lag_steps = jnp.arange(lag_count, dtype=jnp.int32) - lag_count // 2 + NSAMP
    residue = bins[:, None] * lag_steps[None, :] % NSAMP
    angles = 2.0 * math.pi / NSAMP * residue.astype(jnp.float32)
    return jnp.concatenate([jnp.cos(angles), -jnp.sin(angles)], axis=0).astype(jnp.bfloat16)

def apply_whitening(real_part, imag_part, windowed, freq_bins, total_bins, dead_mask, seg_offsets):
    counts = (jnp.minimum(freq_bins + SMOOTH, total_bins - 1) - jnp.maximum(freq_bins - SMOOTH, 0) + 1).astype(jnp.float32)
    smoothed = windowed / counts + EPSILON
    residue = (freq_bins + 1)[None, None, :] * seg_offsets[:, :, None] % NSAMP
    phase = 2.0 * math.pi / NSAMP * residue.astype(jnp.float32)
    scale = dead_mask.astype(jnp.float32)[:, None, None] / smoothed
    cosine = jnp.cos(phase)
    sine = jnp.sin(phase)
    white_real = (real_part * cosine - imag_part * sine) * scale
    white_imag = (real_part * sine + imag_part * cosine) * scale
    return jnp.stack([white_real, white_imag], axis=2).astype(jnp.bfloat16)

def cross_spectra(channels, sources, seg_count):
    chan_real = channels[:, :, 0].astype(jnp.float32)
    chan_imag = channels[:, :, 1].astype(jnp.float32)
    src_real = sources[:, :, 0].astype(jnp.float32)
    src_imag = sources[:, :, 1].astype(jnp.float32)
    cross_real = jnp.einsum('ckf,skf->scf', chan_real, src_real) + jnp.einsum('ckf,skf->scf', chan_imag, src_imag)
    cross_imag = jnp.einsum('ckf,skf->scf', chan_imag, src_real) - jnp.einsum('ckf,skf->scf', chan_real, src_imag)
    joined = jnp.concatenate([cross_real, cross_imag], axis=-1) * (1.0 / math.sqrt(seg_count))
    return joined.astype(jnp.bfloat16)

def reference(spectra, dead_mask, seg_offsets, src_index):
    seg_count = spectra.shape[1]
    total_bins = spectra.shape[3]
    real_part = spectra[:, :, 0].astype(jnp.float32)
    imag_part = spectra[:, :, 1].astype(jnp.float32)
    amplitude = jnp.sqrt(real_part * real_part + imag_part * imag_part)
    padded = jnp.pad(amplitude, ((0, 0), (0, 0), (SMOOTH, SMOOTH)))
    windowed = lax.reduce_window(padded, jnp.zeros((), padded.dtype), lax.add, (1, 1, 2 * SMOOTH + 1), (1, 1, 1), 'VALID')
    freq_bins = jnp.arange(total_bins, dtype=jnp.int32)
    whitened = apply_whitening(real_part, imag_part, windowed, freq_bins, total_bins, dead_mask, seg_offsets)
    panel = whitened[src_index.astype(jnp.int32)]
    table = lag_table(0, total_bins, LAGS)

    def one_source(source):
        spectra_x = cross_spectra(whitened, source[None], seg_count)[0]
        return jnp.dot(spectra_x, table, preferred_element_type=jnp.float32) / math.sqrt(total_bins)
    return lax.map(one_source, panel)
```

```python
import math

import jax
import jax.numpy as jnp
from jax import lax
from jax.experimental import pallas as pl
from jax.experimental.pallas import tpu as pltpu
from jax.sharding import Mesh, PartitionSpec as P

NSAMP = 32768
LAGS = 512
SMOOTH = 64
EPSILON = 1e-06
FREQS = 4096
SLICE = 512
CH = 6
SG = 4
SEGS = 2
LANES = 128


def unit_circle(residue):
    quarter = NSAMP // 4
    quadrant = (residue + quarter // 2) >> 13
    rest = (residue - quadrant * quarter).astype(jnp.float32) * (2.0 * math.pi / NSAMP)
    sq = rest * rest
    sine = rest * (1.0 + sq * (-1.0 / 6 + sq * (1.0 / 120 + sq * (-1.0 / 5040))))
    cosine = 1.0 + sq * (-0.5 + sq * (1.0 / 24 + sq * (-1.0 / 720 + sq * (1.0 / 40320))))
    swap = (quadrant & 1) == 1
    first = jnp.where(swap, sine, cosine)
    second = jnp.where(swap, cosine, sine)
    first = jnp.where(((quadrant + 1) & 2) == 2, -first, first)
    second = jnp.where((quadrant & 2) == 2, -second, second)
    return first, second


def whiten(real, imag, offsets):
    rows = real.shape[0]
    amplitude = jnp.sqrt(real * real + imag * imag)
    edge = jnp.zeros((rows, LANES), jnp.float32)
    padded = jnp.concatenate([edge, amplitude, edge], axis=1)
    width = FREQS + 2 * LANES
    run = padded
    for step in (1, 2, 4, 8, 16, 32, 64):
        run = run + pltpu.roll(run, width - step, 1)
    windowed = pltpu.roll(run, SMOOTH, 1) + pltpu.roll(padded, width - SMOOTH, 1)
    windowed = windowed[:, LANES : LANES + FREQS]
    bins = lax.broadcasted_iota(jnp.int32, (rows, FREQS), 1)
    counts = jnp.minimum(bins + SMOOTH, FREQS - 1) - jnp.maximum(bins - SMOOTH, 0) + 1
    smoothed = windowed / counts.astype(jnp.float32) + EPSILON
    scale = 1.0 / smoothed
    cosine, sine = unit_circle(((bins + 1) * offsets) & (NSAMP - 1))
    white_real = (real * cosine - imag * sine) * scale
    white_imag = (real * sine + imag * cosine) * scale
    return white_real.astype(jnp.bfloat16), white_imag.astype(jnp.bfloat16)


def whiten_sources_kernel(pieces_ref, out_ref):
    parts = [pieces_ref[i] for i in range(FREQS // SLICE)]
    cells = jnp.concatenate([p[:, :SLICE] for p in parts], axis=1).astype(jnp.float32)
    codes = parts[0][:, SLICE : SLICE + LANES].astype(jnp.float32)
    offsets = (codes[0:8] * 256.0 + codes[8:16]).astype(jnp.int32)[:, 0:1]
    real, imag = whiten(cells[0:8], cells[8:16], offsets)
    both = jnp.concatenate([real, imag], axis=0)
    for i in range(out_ref.shape[0]):
        out_ref[i] = both


def whiten_channels_kernel(pieces_ref, offsets_ref, out_ref):
    rows = SEGS * CH
    cells = jnp.concatenate([pieces_ref[i] for i in range(FREQS // SLICE)], axis=1)
    cells = cells.astype(jnp.float32)
    real, imag = whiten(cells[0:rows], cells[rows : 2 * rows], offsets_ref[:, 0:1])
    factor = 1.0 / math.sqrt(SEGS)
    out_ref[0:rows] = real.astype(jnp.float32) * factor
    out_ref[rows : 2 * rows] = imag.astype(jnp.float32) * factor


TABLE_ROWS = 256


def table_kernel(after_ref, out_ref):
    first = pl.program_id(0) * TABLE_ROWS
    shape = (16, LAGS)
    bins = lax.broadcasted_iota(jnp.int32, shape, 0) + 1
    lags = lax.broadcasted_iota(jnp.int32, shape, 1) - LAGS // 2 + NSAMP

    def step(i, carry):
        at = pl.multiple_of(i * 16, 16)
        cosine, sine = unit_circle(((bins + (first + at)) * lags) & (NSAMP - 1))
        out_ref[0, pl.ds(at, 16), :] = cosine.astype(jnp.bfloat16)
        out_ref[1, pl.ds(at, 16), :] = (-sine).astype(jnp.bfloat16)
        return carry

    lax.fori_loop(0, TABLE_ROWS // 16, step, 0)


def halves_sum(first, second, low):
    return jnp.where(low, first, second) + pltpu.roll(jnp.where(low, second, first), 4, 0)


def correlate_kernel(core_ref, mine_ref, other_ref, chan_ref, table_ref, out_ref, cross_ref, sum_ref):
    step = pl.program_id(0)
    low = lax.broadcasted_iota(jnp.int32, (8, LANES), 0) < 4
    for block in range(SLICE // LANES):
        lanes = slice(block * LANES, (block + 1) * LANES)
        chan = []
        for c in range(CH):
            tiles = []
            for q in range(2):
                base = q * SEGS * CH
                one = chan_ref[base + c : base + c + 1, lanes]
                two = chan_ref[base + CH + c : base + CH + c + 1, lanes]
                tiles.append(
                    jnp.where(low, jnp.broadcast_to(one, (8, LANES)), jnp.broadcast_to(two, (8, LANES)))
                )
            chan.append(tiles)
        for half, src_ref in enumerate((mine_ref, other_ref)):
            sources = [src_ref[x, :, lanes].astype(jnp.float32) for x in range(4)]
            for c in range(CH):
                creal, cimag = chan[c]
                reals, imags = [], []
                for x in range(4):
                    sreal, simag = sources[x][0:8], sources[x][8:16]
                    reals.append(creal * sreal + cimag * simag)
                    imags.append(cimag * sreal - creal * simag)
                at = half * CH * 16 + c * 16
                for q, got in enumerate((reals, imags)):
                    rows = jnp.concatenate(
                        [halves_sum(got[0], got[1], low), halves_sum(got[2], got[3], low)], axis=0
                    )
                    cross_ref[q, at : at + 16, lanes] = rows.astype(jnp.bfloat16)
    total = jnp.dot(cross_ref[0], table_ref[0], preferred_element_type=jnp.float32)
    total += jnp.dot(cross_ref[1], table_ref[1], preferred_element_type=jnp.float32)

    @pl.when(step == 0)
    def _():
        sum_ref[...] = total

    @pl.when(step > 0)
    def _():
        sum_ref[...] += total

    @pl.when(step == pl.num_programs(0) - 1)
    def _():
        core = core_ref[0]
        for half in range(2):
            which = core if half == 0 else 1 - core
            for x in range(4):
                for r in range(SG):
                    for c in range(CH):
                        row = half * CH * 16 + c * 16 + x * 4 + r
                        out_ref[x * 8 + which * 4 + r, c : c + 1, :] = sum_ref[row : row + 1, :] * (
                            1.0 / math.sqrt(FREQS)
                        )


def body(spectra, dead_mask, seg_offsets, src_index):
    wide_pos = ((lax.axis_index("y") * 2 + lax.axis_index("h")) * 4 + lax.axis_index("x")) * 2
    wide_pos = wide_pos + lax.axis_index("c")
    alive = spectra * dead_mask.astype(jnp.bfloat16)[:, None, None, None]
    rows = jnp.transpose(alive, (2, 1, 0, 3))
    chan_raw = lax.all_gather(rows.reshape(2 * SEGS * CH, SLICE), "n")

    own = lax.dynamic_slice_in_dim(src_index, wide_pos * SG, SG) - wide_pos * CH
    picked = jnp.zeros((2, SEGS, SG, SLICE), jnp.bfloat16)
    offs = jnp.zeros((SEGS, SG), jnp.int32)
    for c in range(CH):
        hit = own == c
        picked = jnp.where(hit[None, None, :, None], rows[:, :, c : c + 1, :], picked)
        offs = jnp.where(hit[None, :], seg_offsets[c][:, None], offs)
    codes = jnp.stack([offs // 256, offs % 256]).astype(jnp.bfloat16)
    codes = jnp.broadcast_to(codes[..., None], (2, SEGS, SG, LANES))
    payload = jnp.concatenate([picked, codes], axis=-1).reshape(16, SLICE + LANES)

    spread = lax.all_to_all(jnp.broadcast_to(payload[None], (8, 16, SLICE + LANES)), ("y", "h"), 0, 0)
    pieces = lax.all_to_all(spread, "n", 0, 0)

    vmem = pl.BlockSpec(memory_space=pltpu.VMEM)
    white_src = pl.pallas_call(
        whiten_sources_kernel,
        out_shape=jax.ShapeDtypeStruct((4, 16, FREQS), jnp.bfloat16),
        in_specs=[vmem],
        out_specs=vmem,
        compiler_params=pltpu.CompilerParams(vmem_limit_bytes=32 * 2**20),
        name="whiten_sources",
    )(pieces)
    mine = lax.all_to_all(white_src, "x", 0, 0)
    other = lax.ppermute(mine, "c", [(0, 1), (1, 0)])

    table = pl.pallas_call(
        table_kernel,
        grid=(FREQS // TABLE_ROWS,),
        out_shape=jax.ShapeDtypeStruct((2, FREQS, LAGS), jnp.bfloat16),
        in_specs=[pl.BlockSpec((1, 16, LANES), lambda i: (0, 0, 0))],
        out_specs=pl.BlockSpec((2, TABLE_ROWS, LAGS), lambda i: (0, i, 0)),
        compiler_params=pltpu.CompilerParams(vmem_limit_bytes=32 * 2**20),
        cost_estimate=pl.CostEstimate(flops=60 * FREQS * LAGS, bytes_accessed=4 * FREQS * LAGS, transcendentals=0),
        name="lag_table",
    )(spread)

    offsets = jnp.broadcast_to(seg_offsets.T.reshape(SEGS * CH, 1), (SEGS * CH, LANES))
    white_ch = pl.pallas_call(
        whiten_channels_kernel,
        out_shape=jax.ShapeDtypeStruct((2 * SEGS * CH, FREQS), jnp.float32),
        in_specs=[vmem, vmem],
        out_specs=vmem,
        compiler_params=pltpu.CompilerParams(vmem_limit_bytes=32 * 2**20),
        name="whiten_channels",
    )(chan_raw, offsets)

    core = lax.axis_index("c").astype(jnp.int32).reshape(1)
    return pl.pallas_call(
        correlate_kernel,
        grid=(FREQS // SLICE,),
        out_shape=jax.ShapeDtypeStruct((32, CH, LAGS), jnp.float32),
        in_specs=[
            pl.BlockSpec(memory_space=pltpu.SMEM),
            pl.BlockSpec((4, 16, SLICE), lambda i: (0, 0, i)),
            pl.BlockSpec((4, 16, SLICE), lambda i: (0, 0, i)),
            pl.BlockSpec((2 * SEGS * CH, SLICE), lambda i: (0, i)),
            pl.BlockSpec((2, SLICE, LAGS), lambda i: (0, i, 0)),
        ],
        out_specs=pl.BlockSpec((32, CH, LAGS), lambda i: (0, 0, 0)),
        scratch_shapes=[
            pltpu.VMEM((2, 2 * CH * 16, SLICE), jnp.bfloat16),
            pltpu.VMEM((2 * CH * 16, LAGS), jnp.float32),
        ],
        compiler_params=pltpu.CompilerParams(vmem_limit_bytes=40 * 2**20),
        name="correlate",
    )(core, mine, other, white_ch, table)


def solution(mesh):
    parts = Mesh(mesh.devices.reshape(4, 2, 4, 2, 8), ("y", "h", "x", "c", "n"))
    wide = ("y", "h", "x", "c")
    placed = (P(wide, None, None, "n"), P(wide), P(wide, None), P())
    return jax.shard_map(
        body, mesh=parts, in_specs=placed, out_specs=P("n", wide, None), check_vma=False
    )
```

```python
import math

import jax
import jax.numpy as jnp
from jax import lax
from jax.experimental import pallas as pl
from jax.experimental.pallas import tpu as pltpu
from jax.sharding import Mesh, PartitionSpec as P

NSAMP = 32768
LAGS = 512
SMOOTH = 64
EPSILON = 1e-06
FREQS = 4096
SLICE = 512
CH = 6
ROWS = 12
SG = 4
SEGS = 2
LANES = 128


def unit_circle(residue):
    quarter = NSAMP // 4
    quadrant = (residue + quarter // 2) >> 13
    rest = (residue - quadrant * quarter).astype(jnp.float32) * (2.0 * math.pi / NSAMP)
    sq = rest * rest
    sine = rest * (1.0 + sq * (-1.0 / 6 + sq * (1.0 / 120 + sq * (-1.0 / 5040))))
    cosine = 1.0 + sq * (-0.5 + sq * (1.0 / 24 + sq * (-1.0 / 720 + sq * (1.0 / 40320))))
    swap = (quadrant & 1) == 1
    first = jnp.where(swap, sine, cosine)
    second = jnp.where(swap, cosine, sine)
    first = jnp.where(((quadrant + 1) & 2) == 2, -first, first)
    second = jnp.where((quadrant & 2) == 2, -second, second)
    return first, second


def whiten_kernel(
    place_ref, mask_ref, offsets_ref, index_ref, before_ref, own_ref, after_ref, chan_ref, src_ref, keep_ref
):
    own = own_ref[...].astype(jnp.float32)
    before = before_ref[:, SLICE - LANES : SLICE].astype(jnp.float32)
    after = after_ref[:, 0:LANES].astype(jnp.float32)
    cells = jnp.concatenate([before, own, after], axis=1)
    real, imag = cells[0:ROWS], cells[ROWS : 2 * ROWS]
    width = SLICE + 2 * LANES
    amplitude = jnp.sqrt(real * real + imag * imag)
    run = amplitude
    for step in (1, 2, 4, 8, 16, 32, 64):
        run = run + pltpu.roll(run, width - step, 1)
    windowed = pltpu.roll(run, SMOOTH, 1) + pltpu.roll(amplitude, width - SMOOTH, 1)
    windowed = windowed[:, LANES : LANES + SLICE]
    real, imag = real[:, LANES : LANES + SLICE], imag[:, LANES : LANES + SLICE]

    row = lax.broadcasted_iota(jnp.int32, (ROWS, LANES), 0)
    offsets = jnp.zeros((ROWS, LANES), jnp.int32)
    alive = jnp.zeros((ROWS, LANES), jnp.int32)
    for k in range(SEGS):
        for c in range(CH):
            offsets = jnp.where(row == k * CH + c, offsets_ref[c, k], offsets)
            alive = jnp.where(row == k * CH + c, mask_ref[c], alive)
    alive = alive.astype(jnp.float32)
    bins = lax.broadcasted_iota(jnp.int32, (ROWS, SLICE), 1) + place_ref[1] * SLICE
    counts = jnp.minimum(bins + SMOOTH, FREQS - 1) - jnp.maximum(bins - SMOOTH, 0) + 1
    smoothed = windowed / counts.astype(jnp.float32) + EPSILON
    scale = jnp.concatenate([alive] * (SLICE // LANES), axis=1) / smoothed
    wide_offsets = jnp.concatenate([offsets] * (SLICE // LANES), axis=1)
    cosine, sine = unit_circle(((bins + 1) * wide_offsets) & (NSAMP - 1))
    keep_ref[0, 0:ROWS] = (real * cosine - imag * sine) * scale
    keep_ref[1, 0:ROWS] = (real * sine + imag * cosine) * scale

    both = jnp.concatenate([keep_ref[0, 0:ROWS], keep_ref[1, 0:ROWS]], axis=0).astype(jnp.bfloat16)
    for i in range(chan_ref.shape[0]):
        chan_ref[i] = both
    picked = []
    for q in range(2):
        for k in range(SEGS):
            for r in range(SG):
                at = index_ref[place_ref[0] * SG + r] - place_ref[0] * CH + k * CH
                picked.append(keep_ref[q, pl.ds(at, 1), :])
    src_ref[...] = jnp.concatenate(picked, axis=0).astype(jnp.bfloat16)


TABLE_STEPS = 16
INNER = 64


def table_kernel(after_ref, out_ref, inner_ref, outer_ref):
    lags = lax.broadcasted_iota(jnp.int32, (INNER, LAGS), 1) - LAGS // 2 + NSAMP
    row = lax.broadcasted_iota(jnp.int32, (INNER, LAGS), 0)

    @pl.when(pl.program_id(0) == 0)
    def _():
        cosine, sine = unit_circle(((row + 1) * lags) & (NSAMP - 1))
        inner_ref[0], inner_ref[1] = cosine, sine
        cosine, sine = unit_circle((row * INNER * lags) & (NSAMP - 1))
        outer_ref[0], outer_ref[1] = cosine, sine

    per_step = FREQS // INNER // TABLE_STEPS
    for j in range(per_step):
        at = pl.program_id(0) * per_step + j
        ocos, osin = outer_ref[0, pl.ds(at, 1), :], outer_ref[1, pl.ds(at, 1), :]
        for lane in range(LAGS // LANES):
            lanes = slice(lane * LANES, (lane + 1) * LANES)
            wcos = jnp.broadcast_to(ocos[:, lanes], (16, LANES))
            wsin = jnp.broadcast_to(osin[:, lanes], (16, LANES))
            for i in range(INNER // 16):
                rows = slice(i * 16, i * 16 + 16)
                icos, isin = inner_ref[0, rows, lanes], inner_ref[1, rows, lanes]
                put = slice(j * INNER + i * 16, j * INNER + i * 16 + 16)
                out_ref[0, put, lanes] = (icos * wcos - isin * wsin).astype(jnp.bfloat16)
                out_ref[1, put, lanes] = (-(isin * wcos + icos * wsin)).astype(jnp.bfloat16)


def halves_sum(first, second, low):
    return jnp.where(low, first, second) + pltpu.roll(jnp.where(low, second, first), 4, 0)


def correlate_kernel(
    place_ref, mine_ref, other_ref, chan_ref, table_ref, out_ref, wide_ref, cross_ref, sum_ref
):
    step = pl.program_id(0)
    low = lax.broadcasted_iota(jnp.int32, (8, LANES), 0) < 4
    wide_ref[...] = chan_ref[0].astype(jnp.float32) * (1.0 / math.sqrt(SEGS))
    for block in range(SLICE // LANES):
        lanes = slice(block * LANES, (block + 1) * LANES)
        chan = []
        for c in range(CH):
            tiles = []
            for q in range(2):
                base = q * ROWS
                one = wide_ref[base + c : base + c + 1, lanes]
                two = wide_ref[base + CH + c : base + CH + c + 1, lanes]
                tiles.append(
                    jnp.where(low, jnp.broadcast_to(one, (8, LANES)), jnp.broadcast_to(two, (8, LANES)))
                )
            chan.append(tiles)
        for half, src_ref in enumerate((mine_ref, other_ref)):
            sources = [src_ref[0, x, 0, :, lanes].astype(jnp.float32) for x in range(4)]
            for c in range(CH):
                creal, cimag = chan[c]
                reals, imags = [], []
                for x in range(4):
                    sreal, simag = sources[x][0:8], sources[x][8:16]
                    reals.append(creal * sreal + cimag * simag)
                    imags.append(cimag * sreal - creal * simag)
                at = half * CH * 16 + c * 16
                for q, got in enumerate((reals, imags)):
                    rows = jnp.concatenate(
                        [halves_sum(got[0], got[1], low), halves_sum(got[2], got[3], low)], axis=0
                    )
                    cross_ref[q, at : at + 16, lanes] = rows.astype(jnp.bfloat16)
    total = jnp.dot(cross_ref[0], table_ref[0], preferred_element_type=jnp.float32)
    total += jnp.dot(cross_ref[1], table_ref[1], preferred_element_type=jnp.float32)
    total = total.reshape(2, CH, 16, LAGS)

    @pl.when(step == 0)
    def _():
        sum_ref[...] = total

    @pl.when(step > 0)
    def _():
        sum_ref[...] += total

    @pl.when(step == pl.num_programs(0) - 1)
    def _():
        core = place_ref[1]
        for c in range(CH):
            zero, one = sum_ref[core, c], sum_ref[1 - core, c]
            for x in range(4):
                rows = slice(x * 4, x * 4 + 4)
                both = jnp.concatenate([zero[rows], one[rows]], axis=0)
                out_ref[c, x * 8 : x * 8 + 8, :] = both * (1.0 / math.sqrt(FREQS))


def transposed(flip):
    pairs = []
    for y in range(4):
        for h in range(2):
            for n in range(8):
                to_y, to_h, to_n = n // 2, (n % 2) ^ flip, 2 * y + h
                pairs.append(((y * 2 + h) * 8 + n, (to_y * 2 + to_h) * 8 + to_n))
    return pairs


def body(spectra, dead_mask, seg_offsets, src_index):
    pos = {axis: lax.axis_index(axis).astype(jnp.int32) for axis in ("y", "h", "x", "c", "n")}
    wide_pos = ((pos["y"] * 2 + pos["h"]) * 4 + pos["x"]) * 2 + pos["c"]
    rows = jnp.transpose(spectra, (2, 1, 0, 3)).reshape(2 * ROWS, SLICE)
    before = lax.ppermute(rows, "n", [(i, i + 1) for i in range(7)])
    after = lax.ppermute(rows, "n", [(i + 1, i) for i in range(7)])

    vmem = pl.BlockSpec(memory_space=pltpu.VMEM)
    smem = pl.BlockSpec(memory_space=pltpu.SMEM)
    chan_out, src_out = pl.pallas_call(
        whiten_kernel,
        out_shape=(
            jax.ShapeDtypeStruct((8, 2 * ROWS, SLICE), jnp.bfloat16),
            jax.ShapeDtypeStruct((16, SLICE), jnp.bfloat16),
        ),
        in_specs=[smem, smem, smem, smem, vmem, vmem, vmem],
        out_specs=(vmem, vmem),
        scratch_shapes=[pltpu.VMEM((2, 16, SLICE), jnp.float32)],
        compiler_params=pltpu.CompilerParams(vmem_limit_bytes=32 * 2**20),
        name="whiten",
    )(jnp.stack([wide_pos, pos["n"]]), dead_mask, seg_offsets, src_index, before, rows, after)

    moved = [lax.ppermute(src_out, ("y", "h", "n"), transposed(flip)) for flip in range(2)]
    chan_all = lax.all_to_all(chan_out, "n", 0, 0)
    pair = jnp.stack(moved)
    mine = lax.all_to_all(jnp.broadcast_to(pair[None], (16,) + pair.shape), ("y", "x"), 0, 0)
    mine = mine.reshape((4, 4) + pair.shape)
    other = lax.ppermute(mine, "c", [(0, 1), (1, 0)])

    table = pl.pallas_call(
        table_kernel,
        grid=(TABLE_STEPS,),
        out_shape=jax.ShapeDtypeStruct((2, FREQS, LAGS), jnp.bfloat16),
        in_specs=[pl.BlockSpec((16, LANES), lambda i: (0, 0))],
        out_specs=pl.BlockSpec((2, FREQS // TABLE_STEPS, LAGS), lambda i: (0, i, 0)),
        scratch_shapes=[pltpu.VMEM((2, INNER, LAGS), jnp.float32), pltpu.VMEM((2, FREQS // INNER, LAGS), jnp.float32)],
        compiler_params=pltpu.CompilerParams(vmem_limit_bytes=32 * 2**20),
        cost_estimate=pl.CostEstimate(flops=8 * FREQS * LAGS, bytes_accessed=4 * FREQS * LAGS, transcendentals=0),
        name="lag_table",
    )(src_out)

    def source_block(i, place):
        return (i // 2, 0, lax.rem(i + place[0], 2), 0, 0)

    src_spec = pl.BlockSpec((1, 4, 1, 16, SLICE), source_block)
    out = pl.pallas_call(
        correlate_kernel,
        grid_spec=pltpu.PrefetchScalarGridSpec(
            num_scalar_prefetch=1,
            grid=(FREQS // SLICE,),
            in_specs=[
                src_spec,
                src_spec,
                pl.BlockSpec((1, 2 * ROWS, SLICE), lambda i, place: (i, 0, 0)),
                pl.BlockSpec((2, SLICE, LAGS), lambda i, place: (0, i, 0)),
            ],
            out_specs=pl.BlockSpec((CH, 32, LAGS), lambda i, place: (0, 0, 0)),
            scratch_shapes=[
                pltpu.VMEM((2 * ROWS, SLICE), jnp.float32),
                pltpu.VMEM((2, 2 * CH * 16, SLICE), jnp.bfloat16),
                pltpu.VMEM((2, CH, 16, LAGS), jnp.float32),
            ],
        ),
        out_shape=jax.ShapeDtypeStruct((CH, 32, LAGS), jnp.float32),
        compiler_params=pltpu.CompilerParams(vmem_limit_bytes=40 * 2**20),
        name="correlate",
    )(jnp.stack([pos["h"], pos["c"]]), mine, other, chan_all, table)
    return jnp.transpose(out, (1, 0, 2))


def solution(mesh):
    parts = Mesh(mesh.devices.reshape(4, 2, 4, 2, 8), ("y", "h", "x", "c", "n"))
    wide = ("y", "h", "x", "c")
    placed = (P(wide, None, None, "n"), P(wide), P(wide, None), P())
    return jax.shard_map(
        body, mesh=parts, in_specs=placed, out_specs=P("n", wide, None), check_vma=False
    )
```

```python
import math

import jax
import jax.numpy as jnp
from jax import lax
from jax.experimental import pallas as pl
from jax.experimental.pallas import tpu as pltpu
from jax.sharding import Mesh, PartitionSpec as P

NSAMP = 32768
LAGS = 512
SMOOTH = 64
EPSILON = 1e-06
FREQS = 4096
SLICE = 512
CH = 6
ROWS = 12
SG = 4
SEGS = 2
LANES = 128
QUARTER = FREQS // 4
INDEX_AT = 2 + CH + SEGS * CH


def unit_circle(residue):
    quarter = NSAMP // 4
    quadrant = (residue + quarter // 2) >> 13
    rest = (residue - quadrant * quarter).astype(jnp.float32) * (2.0 * math.pi / NSAMP)
    sq = rest * rest
    sine = rest * (1.0 + sq * (-1.0 / 6 + sq * (1.0 / 120 + sq * (-1.0 / 5040))))
    cosine = 1.0 + sq * (-0.5 + sq * (1.0 / 24 + sq * (-1.0 / 720 + sq * (1.0 / 40320))))
    swap = (quadrant & 1) == 1
    first = jnp.where(swap, sine, cosine)
    second = jnp.where(swap, cosine, sine)
    first = jnp.where(((quadrant + 1) & 2) == 2, -first, first)
    second = jnp.where((quadrant & 2) == 2, -second, second)
    return first, second


NEAR = ("42601375", "35710264", "20643157", "02175346", "13420657", "02643175", "31576024", "20467153")


def whiten_kernel(info_ref, pieces_ref, chan_ref, src_ref, keep_ref):
    block, place = info_ref[0], info_ref[1]
    cells = jnp.concatenate([pieces_ref[i] for i in range(FREQS // SLICE)], axis=1).astype(jnp.float32)
    real, imag = cells[0:ROWS], cells[ROWS : 2 * ROWS]
    amplitude = jnp.sqrt(real * real + imag * imag)
    edge = jnp.zeros((ROWS, LANES), jnp.float32)
    padded = jnp.concatenate([edge, amplitude, edge], axis=1)
    width = FREQS + 2 * LANES
    run = padded
    for step in (1, 2, 4, 8, 16, 32, 64):
        run = run + pltpu.roll(run, width - step, 1)
    windowed = pltpu.roll(run, SMOOTH, 1) + pltpu.roll(padded, width - SMOOTH, 1)
    windowed = windowed[:, LANES : LANES + FREQS]

    row = lax.broadcasted_iota(jnp.int32, (ROWS, LANES), 0)
    offsets = jnp.zeros((ROWS, LANES), jnp.int32)
    alive = jnp.zeros((ROWS, LANES), jnp.int32)
    for k in range(SEGS):
        for c in range(CH):
            offsets = jnp.where(row == k * CH + c, info_ref[2 + CH + k * CH + c], offsets)
            alive = jnp.where(row == k * CH + c, info_ref[2 + c], alive)
    alive = alive.astype(jnp.float32)
    bins = lax.broadcasted_iota(jnp.int32, (ROWS, FREQS), 1)
    counts = jnp.minimum(bins + SMOOTH, FREQS - 1) - jnp.maximum(bins - SMOOTH, 0) + 1
    smoothed = windowed / counts.astype(jnp.float32) + EPSILON
    scale = jnp.concatenate([alive] * (FREQS // LANES), axis=1) / smoothed
    wide_offsets = jnp.concatenate([offsets] * (FREQS // LANES), axis=1)
    cosine, sine = unit_circle(((bins + 1) * wide_offsets) & (NSAMP - 1))
    white = [
        ((real * cosine - imag * sine) * scale).astype(jnp.bfloat16).astype(jnp.float32),
        ((real * sine + imag * cosine) * scale).astype(jnp.bfloat16).astype(jnp.float32),
    ]
    for q in range(2):
        for i in range(4):
            keep_ref[i, q, 0:ROWS] = white[q][:, i * QUARTER : (i + 1) * QUARTER]
    both = jnp.concatenate(white, axis=0) * (1.0 / math.sqrt(SEGS))
    for i in range(FREQS // SLICE):
        chan_ref[i] = both[:, i * SLICE : (i + 1) * SLICE]

    code = jnp.int32(0)
    for group, line in enumerate(NEAR):
        packed = sum((int(to) // 2) << (2 * n) for n, to in enumerate(line))
        code = jnp.where(block // 8 == group, packed, code)
    quarter = (code >> (2 * place)) & 3
    picked = []
    for q in range(2):
        for k in range(SEGS):
            for r in range(SG):
                at = info_ref[INDEX_AT + block * SG + r] - block * CH + k * CH
                picked.append(keep_ref[quarter, q, pl.ds(at, 1), :])
    src_ref[...] = jnp.concatenate(picked, axis=0).astype(jnp.bfloat16)


INNER = 64


def halves_sum(first, second, low):
    return jnp.where(low, first, second) + pltpu.roll(jnp.where(low, second, first), 4, 0)


HALF = LAGS // 2
PAIRS = 2 * CH * 16


def correlate_kernel(
    core_ref, mine_ref, other_ref, chan_ref, out_ref,
    inner_ref, outer_ref, even_cross, odd_cross, even_table, odd_table, cos_sum, sin_sum, last_sum, sum_ref
):
    low = lax.broadcasted_iota(jnp.int32, (8, LANES), 0) < 4
    lane = lax.broadcasted_iota(jnp.int32, (INNER, LAGS), 1)
    lags = jnp.where(lane < HALF, lane, lane - (HALF - 1))
    row = lax.broadcasted_iota(jnp.int32, (INNER, LAGS), 0)
    inner_ref[0], inner_ref[1] = unit_circle(((row + 1) * lags) & (NSAMP - 1))
    outer_ref[0], outer_ref[1] = unit_circle((row * INNER * lags) & (NSAMP - 1))

    def make_table(step, table_ref):
        for u in range(SLICE // INNER):
            at = step * (SLICE // INNER) + u
            ocos, osin = outer_ref[0, pl.ds(at, 1), :], outer_ref[1, pl.ds(at, 1), :]
            for block in range(LAGS // LANES):
                lanes = slice(block * LANES, (block + 1) * LANES)
                wcos = jnp.broadcast_to(ocos[:, lanes], (16, LANES))
                wsin = jnp.broadcast_to(osin[:, lanes], (16, LANES))
                for i in range(INNER // 16):
                    rows = slice(i * 16, i * 16 + 16)
                    icos, isin = inner_ref[0, rows, lanes], inner_ref[1, rows, lanes]
                    if block * LANES < HALF:
                        value = icos * wcos - isin * wsin
                    else:
                        value = isin * wcos + icos * wsin
                    put = u * INNER + i * 16
                    table_ref[put : put + 16, lanes] = value.astype(jnp.bfloat16)

    def cross(quarter, part, cross_ref):
        step = 2 * quarter + part
        for block in range(SLICE // LANES):
            lanes = slice(block * LANES, (block + 1) * LANES)
            from_lanes = slice(part * SLICE + block * LANES, part * SLICE + (block + 1) * LANES)
            chan = []
            for c in range(CH):
                tiles = []
                for q in range(2):
                    base = q * ROWS
                    one = chan_ref[step, base + c : base + c + 1, lanes]
                    two = chan_ref[step, base + CH + c : base + CH + c + 1, lanes]
                    tiles.append(
                        jnp.where(low, jnp.broadcast_to(one, (8, LANES)), jnp.broadcast_to(two, (8, LANES)))
                    )
                chan.append(tiles)
            for half, src_ref in enumerate((mine_ref, other_ref)):
                sources = [src_ref[quarter, x, :, from_lanes].astype(jnp.float32) for x in range(4)]
                for c in range(CH):
                    creal, cimag = chan[c]
                    reals, imags = [], []
                    for x in range(4):
                        sreal, simag = sources[x][0:8], sources[x][8:16]
                        reals.append(creal * sreal + cimag * simag)
                        imags.append(cimag * sreal - creal * simag)
                    at = half * CH * 16 + c * 16
                    for q, got in enumerate((reals, imags)):
                        rows = jnp.concatenate(
                            [halves_sum(got[0], got[1], low), halves_sum(got[2], got[3], low)], axis=0
                        ).astype(jnp.bfloat16)
                        cross_ref[q, at : at + 16, lanes] = rows
                        if q == 0:
                            last_sum[at : at + 16] += rows.astype(jnp.float32)

    def add(cross_ref, table_ref):
        cos_sum[...] += jnp.dot(cross_ref[0], table_ref[:, :HALF], preferred_element_type=jnp.float32)
        sin_sum[...] += jnp.dot(cross_ref[1], table_ref[:, HALF:], preferred_element_type=jnp.float32)

    cos_sum[...] = jnp.zeros_like(cos_sum)
    sin_sum[...] = jnp.zeros_like(sin_sum)
    last_sum[...] = jnp.zeros_like(last_sum)
    steps = FREQS // SLICE
    make_table(0, even_table)
    cross(0, 0, even_cross)

    def pair(i, carry):
        make_table(2 * i + 1, odd_table)
        cross(i, 1, odd_cross)
        add(even_cross, even_table)
        make_table(2 * i + 2, even_table)
        cross(i + 1, 0, even_cross)
        add(odd_cross, odd_table)
        return carry

    lax.fori_loop(0, steps // 2 - 1, pair, 0)
    make_table(steps - 1, odd_table)
    cross(steps // 2 - 1, 1, odd_cross)
    add(even_cross, even_table)
    add(odd_cross, odd_table)

    period = lax.broadcasted_iota(jnp.int32, (8, LANES), 1) + 1
    wave = unit_circle((period * HALF) & (NSAMP - 1))[0].astype(jnp.bfloat16).astype(jnp.float32)
    cos_last = jnp.sum(last_sum[...] * wave[0:1], axis=1, keepdims=True)
    cosines, sines = cos_sum[...], sin_sum[...]
    lane = lax.broadcasted_iota(jnp.int32, (PAIRS, HALF), 1)
    positive = cosines - jnp.where(lane == 0, 0.0, pltpu.roll(sines, 1, 1))
    negative = jnp.where(lane == HALF - 1, cos_last, pltpu.roll(cosines, HALF - 1, 1)) + sines
    first = negative.astype(jnp.bfloat16)
    rest = negative - first.astype(jnp.float32)
    second = rest.astype(jnp.bfloat16)
    third = (rest - second.astype(jnp.float32)).astype(jnp.bfloat16)
    mirror = (
        lax.broadcasted_iota(jnp.int32, (HALF, HALF), 0) + lax.broadcasted_iota(jnp.int32, (HALF, HALF), 1)
        == HALF - 1
    ).astype(jnp.float32).astype(jnp.bfloat16)
    flipped = [jnp.dot(t, mirror, preferred_element_type=jnp.float32) for t in (first, second, third)]
    factor = 1.0 / math.sqrt(FREQS)
    sum_ref[:, :, :, :HALF] = ((flipped[0] + flipped[1] + flipped[2]) * factor).reshape(2, CH, 16, HALF)
    sum_ref[:, :, :, HALF:] = (positive * factor).reshape(2, CH, 16, HALF)

    core = core_ref[0]
    for c in range(CH):
        zero, one = sum_ref[core, c], sum_ref[1 - core, c]
        for x in range(4):
            rows = slice(x * 4, x * 4 + 4)
            out_ref[c, x * 8 : x * 8 + 8, :] = jnp.concatenate([zero[rows], one[rows]], axis=0)


def scattered():
    pairs = []
    for group in range(8):
        for n in range(8):
            pairs.append((group * 8 + n, int(NEAR[group][n]) * 8 + group))
    return pairs


def body(spectra, dead_mask, seg_offsets, src_index):
    pos = {axis: lax.axis_index(axis).astype(jnp.int32) for axis in ("y", "h", "x", "c", "n")}
    wide_pos = ((pos["y"] * 2 + pos["h"]) * 4 + pos["x"]) * 2 + pos["c"]
    rows = jnp.transpose(spectra, (2, 1, 0, 3)).reshape(2 * ROWS, SLICE)
    info = jnp.concatenate(
        [jnp.stack([wide_pos, pos["n"]]), dead_mask, seg_offsets.T.reshape(SEGS * CH), src_index]
    )
    rows, info = lax.optimization_barrier((rows, info))
    pieces = lax.all_to_all(jnp.broadcast_to(rows[None], (8, 2 * ROWS, SLICE)), "n", 0, 0)

    vmem = pl.BlockSpec(memory_space=pltpu.VMEM)
    smem = pl.BlockSpec(memory_space=pltpu.SMEM)
    chan, src_out = pl.pallas_call(
        whiten_kernel,
        out_shape=(
            jax.ShapeDtypeStruct((FREQS // SLICE, 2 * ROWS, SLICE), jnp.float32),
            jax.ShapeDtypeStruct((16, QUARTER), jnp.bfloat16),
        ),
        in_specs=[smem, vmem],
        out_specs=(vmem, vmem),
        scratch_shapes=[pltpu.VMEM((4, 2, 16, QUARTER), jnp.float32)],
        compiler_params=pltpu.CompilerParams(vmem_limit_bytes=32 * 2**20),
        name="whiten",
    )(info, pieces)

    moved = lax.ppermute(src_out, ("y", "h", "n"), scattered())
    mine = lax.all_to_all(jnp.broadcast_to(moved[None], (16,) + moved.shape), ("y", "x"), 0, 0)
    mine = mine.reshape((4, 4) + moved.shape)
    other = lax.ppermute(mine, "c", [(0, 1), (1, 0)])

    out = pl.pallas_call(
        correlate_kernel,
        in_specs=[smem, vmem, vmem, vmem],
        out_specs=vmem,
        scratch_shapes=[
            pltpu.VMEM((2, INNER, LAGS), jnp.float32),
            pltpu.VMEM((2, FREQS // INNER, LAGS), jnp.float32),
            pltpu.VMEM((2, PAIRS, SLICE), jnp.bfloat16),
            pltpu.VMEM((2, PAIRS, SLICE), jnp.bfloat16),
            pltpu.VMEM((SLICE, LAGS), jnp.bfloat16),
            pltpu.VMEM((SLICE, LAGS), jnp.bfloat16),
            pltpu.VMEM((PAIRS, HALF), jnp.float32),
            pltpu.VMEM((PAIRS, HALF), jnp.float32),
            pltpu.VMEM((PAIRS, LANES), jnp.float32),
            pltpu.VMEM((2, CH, 16, LAGS), jnp.float32),
        ],
        out_shape=jax.ShapeDtypeStruct((CH, 32, LAGS), jnp.float32),
        compiler_params=pltpu.CompilerParams(vmem_limit_bytes=20 * 2**20),
        name="correlate",
    )(pos["c"].reshape(1), mine, other, chan)
    return jnp.transpose(out, (1, 0, 2))


def solution(mesh):
    parts = Mesh(mesh.devices.reshape(4, 2, 4, 2, 8), ("y", "h", "x", "c", "n"))
    wide = ("y", "h", "x", "c")
    placed = (P(wide, None, None, "n"), P(wide), P(wide, None), P())
    return jax.shard_map(
        body, mesh=parts, in_specs=placed, out_specs=P("n", wide, None), check_vma=False
    )
```

```python
import math

import jax
import jax.numpy as jnp
from jax import lax
from jax.experimental import pallas as pl
from jax.experimental.pallas import tpu as pltpu
from jax.sharding import Mesh, PartitionSpec as P

NSAMP = 32768
LAGS = 512
SMOOTH = 64
EPSILON = 1e-06
FREQS = 4096
SLICE = 512
CH = 6
ROWS = 12
SG = 4
SEGS = 2
LANES = 128
QUARTER = FREQS // 4


def unit_circle(residue):
    quarter = NSAMP // 4
    quadrant = (residue + quarter // 2) >> 13
    rest = (residue - quadrant * quarter).astype(jnp.float32) * (2.0 * math.pi / NSAMP)
    sq = rest * rest
    sine = rest * (1.0 + sq * (-1.0 / 6 + sq * (1.0 / 120 + sq * (-1.0 / 5040))))
    cosine = 1.0 + sq * (-0.5 + sq * (1.0 / 24 + sq * (-1.0 / 720 + sq * (1.0 / 40320))))
    swap = (quadrant & 1) == 1
    first = jnp.where(swap, sine, cosine)
    second = jnp.where(swap, cosine, sine)
    first = jnp.where(((quadrant + 1) & 2) == 2, -first, first)
    second = jnp.where((quadrant & 2) == 2, -second, second)
    return first, second


def turned(pair, by):
    return pair[0] * by[0] - pair[1] * by[1], pair[1] * by[0] + pair[0] * by[1]


NEAR = ("42601375", "35710264", "20643157", "02175346", "13420657", "02643175", "31576024", "20467153")


def whiten_kernel(info_ref, pieces_ref, chan_ref, src_ref, keep_ref):
    block, place = info_ref[4, 0], info_ref[4, 1]
    cells = jnp.concatenate([pieces_ref[i] for i in range(FREQS // SLICE)], axis=1).astype(jnp.float32)
    real, imag = cells[0:ROWS], cells[ROWS : 2 * ROWS]
    amplitude = jnp.sqrt(real * real + imag * imag)
    edge = jnp.zeros((ROWS, LANES), jnp.float32)
    padded = jnp.concatenate([edge, amplitude, edge], axis=1)
    width = FREQS + 2 * LANES
    run = padded
    for step in (1, 2, 4, 8, 16, 32, 64):
        run = run + pltpu.roll(run, width - step, 1)
    windowed = pltpu.roll(run, SMOOTH, 1) + pltpu.roll(padded, width - SMOOTH, 1)
    windowed = windowed[:, LANES : LANES + FREQS]

    row = lax.broadcasted_iota(jnp.int32, (ROWS, LANES), 0)
    offsets = jnp.zeros((ROWS, LANES), jnp.int32)
    alive = jnp.zeros((ROWS, LANES), jnp.int32)
    for k in range(SEGS):
        for c in range(CH):
            offsets = jnp.where(row == k * CH + c, info_ref[1 + k, c], offsets)
            alive = jnp.where(row == k * CH + c, info_ref[3, c], alive)
    alive = alive.astype(jnp.float32)
    lane = lax.broadcasted_iota(jnp.int32, (ROWS, LANES), 1)
    head = windowed[:, :LANES] / (jnp.minimum(lane, SMOOTH) + (SMOOTH + 1)).astype(jnp.float32)
    tail = windowed[:, FREQS - LANES :] / (
        jnp.minimum(LANES - 1 - lane, SMOOTH) + (SMOOTH + 1)
    ).astype(jnp.float32)
    middle = windowed[:, LANES : FREQS - LANES] * (1.0 / (2 * SMOOTH + 1))
    smoothed = jnp.concatenate([head, middle, tail], axis=1) + EPSILON
    scale = jnp.concatenate([alive] * (FREQS // LANES), axis=1) / smoothed

    inner = unit_circle(((lane + 1) * offsets) & (NSAMP - 1))
    groups = [inner]
    for j in (1, 2, 3):
        groups.append(turned(inner, unit_circle((j * LANES * offsets) & (NSAMP - 1))))
    angles = list(groups)
    for j in range(1, FREQS // (4 * LANES)):
        outer = unit_circle((j * 4 * LANES * offsets) & (NSAMP - 1))
        angles += [turned(group, outer) for group in groups]
    cosine = jnp.concatenate([pair[0] for pair in angles], axis=1)
    sine = jnp.concatenate([pair[1] for pair in angles], axis=1)
    white = [
        ((real * cosine - imag * sine) * scale).astype(jnp.bfloat16).astype(jnp.float32),
        ((real * sine + imag * cosine) * scale).astype(jnp.bfloat16).astype(jnp.float32),
    ]
    for q in range(2):
        for i in range(4):
            keep_ref[i, q, 0:ROWS] = white[q][:, i * QUARTER : (i + 1) * QUARTER]
        scaled = white[q] * (1.0 / math.sqrt(SEGS))
        for i in range(FREQS // SLICE):
            chan_ref[i, q] = scaled[:, i * SLICE : (i + 1) * SLICE]

    code = jnp.int32(0)
    for group, line in enumerate(NEAR):
        packed = sum((int(to) // 2) << (2 * n) for n, to in enumerate(line))
        code = jnp.where(block // 8 == group, packed, code)
    quarter = (code >> (2 * place)) & 3
    picked = []
    for q in range(2):
        for k in range(SEGS):
            for r in range(SG):
                at = info_ref[0, block * SG + r] - block * CH + k * CH
                picked.append(keep_ref[quarter, q, pl.ds(at, 1), :])
    src_ref[...] = jnp.concatenate(picked, axis=0).astype(jnp.bfloat16)


INNER = 64


HALF = LAGS // 2
PAIRS = 2 * CH * 16


def table_kernel(after_ref, table_ref, inner_ref, outer_ref):
    lane = lax.broadcasted_iota(jnp.int32, (INNER, LAGS), 1)
    lags = jnp.where(lane < HALF, lane, lane - (HALF - 1))
    row = lax.broadcasted_iota(jnp.int32, (INNER, LAGS), 0)
    inner_ref[0], inner_ref[1] = unit_circle(((row + 1) * lags) & (NSAMP - 1))
    for q, values in enumerate(unit_circle((row * INNER * lags) & (NSAMP - 1))):
        for block in range(LAGS // LANES):
            outer_ref[q, block] = values[:, block * LANES : (block + 1) * LANES]
    for block in range(LAGS // LANES):
        lanes = slice(block * LANES, (block + 1) * LANES)
        for i in range(INNER // 16):
            rows = slice(i * 16, i * 16 + 16)
            icos, isin = inner_ref[0, rows, lanes], inner_ref[1, rows, lanes]

            def put(at, carry, icos=icos, isin=isin, block=block, lanes=lanes, i=i):
                wcos = jnp.broadcast_to(outer_ref[0, block, pl.ds(at, 1), :], (16, LANES))
                wsin = jnp.broadcast_to(outer_ref[1, block, pl.ds(at, 1), :], (16, LANES))
                if lanes.start < HALF:
                    value = icos * wcos - isin * wsin
                else:
                    value = isin * wcos + icos * wsin
                table_ref[at, i * 16 : i * 16 + 16, lanes] = value.astype(jnp.bfloat16)
                return carry

            lax.fori_loop(0, FREQS // INNER, put, 0, unroll=16)


def correlate_kernel(
    core_ref, mine_ref, other_ref, chan_ref, table_ref, out_ref,
    even_cross, odd_cross, cos_sum, sin_sum, last_sum, sum_ref
):
    low = lax.broadcasted_iota(jnp.int32, (8, LANES), 0) < 4

    def cross(quarter, part, cross_ref):
        step = 2 * quarter + part
        for block in range(SLICE // LANES):
            lanes = slice(block * LANES, (block + 1) * LANES)
            from_lanes = slice(part * SLICE + block * LANES, part * SLICE + (block + 1) * LANES)
            for half, src_ref in enumerate((mine_ref, other_ref)):
                tiles = []
                for x in (0, 2):
                    first = src_ref[quarter, x, :, from_lanes].astype(jnp.float32)
                    second = src_ref[quarter, x + 1, :, from_lanes].astype(jnp.float32)
                    parts = []
                    for q in range(2):
                        one, two = first[q * 8 : q * 8 + 8], second[q * 8 : q * 8 + 8]
                        parts.append(jnp.where(low, one, pltpu.roll(two, 4, 0)))
                        parts.append(jnp.where(low, pltpu.roll(one, 4, 0), two))
                    tiles.append(parts)
                for c in range(CH):
                    creal, cimag = [
                        [
                            jnp.broadcast_to(
                                chan_ref[step, q, k * CH + c : k * CH + c + 1, lanes],
                                (8, LANES),
                            )
                            for k in range(SEGS)
                        ]
                        for q in range(2)
                    ]
                    reals, imags = [], []
                    for real0, real1, imag0, imag1 in tiles:
                        reals.append(
                            (creal[0] * real0 + cimag[0] * imag0) + (creal[1] * real1 + cimag[1] * imag1)
                        )
                        imags.append(
                            (cimag[0] * real0 - creal[0] * imag0) + (cimag[1] * real1 - creal[1] * imag1)
                        )
                    at = half * CH * 16 + c * 16
                    for q, got in enumerate((reals, imags)):
                        rows = jnp.concatenate(got, axis=0).astype(jnp.bfloat16)
                        cross_ref[q, at : at + 16, lanes] = rows
                        if q == 0:
                            last_sum[at : at + 16] += rows.astype(jnp.float32)

    def add(step, cross_ref):
        chunk = table_ref[pl.ds(step * (SLICE // INNER), SLICE // INNER)].reshape(SLICE, LAGS)
        cos_sum[...] += jnp.dot(cross_ref[0], chunk[:, :HALF], preferred_element_type=jnp.float32)
        sin_sum[...] += jnp.dot(cross_ref[1], chunk[:, HALF:], preferred_element_type=jnp.float32)

    cos_sum[...] = jnp.zeros_like(cos_sum)
    sin_sum[...] = jnp.zeros_like(sin_sum)
    last_sum[...] = jnp.zeros_like(last_sum)
    steps = FREQS // SLICE
    cross(0, 0, even_cross)

    def pair(i, carry):
        cross(i, 1, odd_cross)
        add(2 * i, even_cross)
        cross(i + 1, 0, even_cross)
        add(2 * i + 1, odd_cross)
        return carry

    lax.fori_loop(0, steps // 2 - 1, pair, 0)
    cross(steps // 2 - 1, 1, odd_cross)
    add(steps - 2, even_cross)
    add(steps - 1, odd_cross)

    period = lax.broadcasted_iota(jnp.int32, (8, LANES), 1) + 1
    wave = unit_circle((period * HALF) & (NSAMP - 1))[0].astype(jnp.bfloat16).astype(jnp.float32)
    cos_last = jnp.sum(last_sum[...] * wave[0:1], axis=1, keepdims=True)
    cosines, sines = cos_sum[...], sin_sum[...]
    lane = lax.broadcasted_iota(jnp.int32, (PAIRS, HALF), 1)
    positive = cosines - jnp.where(lane == 0, 0.0, pltpu.roll(sines, 1, 1))
    negative = jnp.where(lane == HALF - 1, cos_last, pltpu.roll(cosines, HALF - 1, 1)) + sines
    first = negative.astype(jnp.bfloat16)
    rest = negative - first.astype(jnp.float32)
    second = rest.astype(jnp.bfloat16)
    third = (rest - second.astype(jnp.float32)).astype(jnp.bfloat16)
    mirror = (
        lax.broadcasted_iota(jnp.int32, (HALF, HALF), 0) + lax.broadcasted_iota(jnp.int32, (HALF, HALF), 1)
        == HALF - 1
    ).astype(jnp.float32).astype(jnp.bfloat16)
    flipped = [jnp.dot(t, mirror, preferred_element_type=jnp.float32) for t in (first, second, third)]
    factor = 1.0 / math.sqrt(FREQS)
    sum_ref[:, :, :, :HALF] = ((flipped[0] + flipped[1] + flipped[2]) * factor).reshape(2, CH, 16, HALF)
    sum_ref[:, :, :, HALF:] = (positive * factor).reshape(2, CH, 16, HALF)

    core = core_ref[0]
    for c in range(CH):
        zero, one = sum_ref[core, c], sum_ref[1 - core, c]
        for x in range(4):
            rows = slice(x * 4, x * 4 + 4)
            out_ref[c, x * 8 : x * 8 + 8, :] = jnp.concatenate([zero[rows], one[rows]], axis=0)


def scattered():
    pairs = []
    for group in range(8):
        for n in range(8):
            pairs.append((group * 8 + n, int(NEAR[group][n]) * 8 + group))
    return pairs


def body(spectra, dead_mask, seg_offsets, src_index):
    pos = {axis: lax.axis_index(axis).astype(jnp.int32) for axis in ("y", "h", "x", "c", "n")}
    wide_pos = ((pos["y"] * 2 + pos["h"]) * 4 + pos["x"]) * 2 + pos["c"]
    rows = jnp.transpose(spectra, (2, 1, 0, 3)).reshape(2 * ROWS, SLICE)
    width = src_index.shape[0]
    info = jnp.concatenate(
        [
            src_index[None],
            jnp.pad(seg_offsets.T, ((0, 0), (0, width - CH))),
            jnp.pad(dead_mask, (0, width - CH))[None],
            jnp.pad(jnp.stack([wide_pos, pos["n"]]), (0, width - 2))[None],
        ]
    )
    pieces = lax.all_to_all(jnp.broadcast_to(rows[None], (8, 2 * ROWS, SLICE)), "n", 0, 0)

    vmem = pl.BlockSpec(memory_space=pltpu.VMEM)
    smem = pl.BlockSpec(memory_space=pltpu.SMEM)
    chan, src_out = pl.pallas_call(
        whiten_kernel,
        out_shape=(
            jax.ShapeDtypeStruct((FREQS // SLICE, 2, ROWS, SLICE), jnp.float32),
            jax.ShapeDtypeStruct((16, QUARTER), jnp.bfloat16),
        ),
        in_specs=[smem, vmem],
        out_specs=(vmem, vmem),
        scratch_shapes=[pltpu.VMEM((4, 2, 16, QUARTER), jnp.float32)],
        compiler_params=pltpu.CompilerParams(vmem_limit_bytes=32 * 2**20),
        name="whiten",
    )(info, pieces)

    moved = lax.ppermute(src_out, ("y", "h", "n"), scattered())
    mine = lax.all_to_all(jnp.broadcast_to(moved[None], (16,) + moved.shape), ("y", "x"), 0, 0)
    mine = mine.reshape((4, 4) + moved.shape)
    other = lax.ppermute(mine, "c", [(0, 1), (1, 0)])

    table = pl.pallas_call(
        table_kernel,
        in_specs=[pl.BlockSpec(memory_space=pl.ANY)],
        out_specs=vmem,
        scratch_shapes=[
            pltpu.VMEM((2, INNER, LAGS), jnp.float32),
            pltpu.VMEM((2, LAGS // LANES, FREQS // INNER, LANES), jnp.float32),
        ],
        out_shape=jax.ShapeDtypeStruct((FREQS // INNER, INNER, LAGS), jnp.bfloat16),
        compiler_params=pltpu.CompilerParams(vmem_limit_bytes=16 * 2**20),
        cost_estimate=pl.CostEstimate(flops=4 * FREQS * LAGS, bytes_accessed=2 * FREQS * LAGS, transcendentals=0),
        name="lag_table",
    )(mine)

    out = pl.pallas_call(
        correlate_kernel,
        in_specs=[smem, vmem, vmem, vmem, vmem],
        out_specs=vmem,
        scratch_shapes=[
            pltpu.VMEM((2, PAIRS, SLICE), jnp.bfloat16),
            pltpu.VMEM((2, PAIRS, SLICE), jnp.bfloat16),
            pltpu.VMEM((PAIRS, HALF), jnp.float32),
            pltpu.VMEM((PAIRS, HALF), jnp.float32),
            pltpu.VMEM((PAIRS, LANES), jnp.float32),
            pltpu.VMEM((2, CH, 16, LAGS), jnp.float32),
        ],
        out_shape=jax.ShapeDtypeStruct((CH, 32, LAGS), jnp.float32),
        compiler_params=pltpu.CompilerParams(vmem_limit_bytes=20 * 2**20),
        name="correlate",
    )(pos["c"].reshape(1), mine, other, chan, table)
    return jnp.transpose(out, (1, 0, 2))


def solution(mesh):
    parts = Mesh(mesh.devices.reshape(4, 2, 4, 2, 8), ("y", "h", "x", "c", "n"))
    wide = ("y", "h", "x", "c")
    placed = (P(wide, None, None, "n"), P(wide), P(wide, None), P())
    return jax.shard_map(
        body, mesh=parts, in_specs=placed, out_specs=P("n", wide, None), check_vma=False
    )
```

```python
import math

import jax
import jax.numpy as jnp
from jax import lax
from jax.experimental import pallas as pl
from jax.experimental.pallas import tpu as pltpu
from jax.sharding import Mesh, PartitionSpec as P

NSAMP = 32768
LAGS = 512
SMOOTH = 64
EPSILON = 1e-06
FREQS = 4096
SLICE = 512
CH = 6
ROWS = 12
SG = 4
SEGS = 2
LANES = 128
SHARE = FREQS // 2


def unit_circle(residue):
    quarter = NSAMP // 4
    quadrant = (residue + quarter // 2) >> 13
    rest = (residue - quadrant * quarter).astype(jnp.float32) * (2.0 * math.pi / NSAMP)
    sq = rest * rest
    sine = rest * (1.0 + sq * (-1.0 / 6 + sq * (1.0 / 120 + sq * (-1.0 / 5040))))
    cosine = 1.0 + sq * (-0.5 + sq * (1.0 / 24 + sq * (-1.0 / 720 + sq * (1.0 / 40320))))
    swap = (quadrant & 1) == 1
    first = jnp.where(swap, sine, cosine)
    second = jnp.where(swap, cosine, sine)
    first = jnp.where(((quadrant + 1) & 2) == 2, -first, first)
    second = jnp.where((quadrant & 2) == 2, -second, second)
    return first, second


def turned(pair, by):
    return pair[0] * by[0] - pair[1] * by[1], pair[1] * by[0] + pair[0] * by[1]


NEAR = ("42601375", "35710264", "20643157", "02175346", "13420657", "02643175", "31576024", "20467153")


def whiten_kernel(info_ref, pieces_ref, chan_ref, src_ref, keep_ref):
    block, place = info_ref[4, 0], info_ref[4, 1]
    cells = jnp.concatenate([pieces_ref[i] for i in range(FREQS // SLICE)], axis=1).astype(jnp.float32)
    real, imag = cells[0:ROWS], cells[ROWS : 2 * ROWS]
    amplitude = jnp.sqrt(real * real + imag * imag)
    edge = jnp.zeros((ROWS, LANES), jnp.float32)
    padded = jnp.concatenate([edge, amplitude, edge], axis=1)
    width = FREQS + 2 * LANES
    run = padded
    for step in (1, 2, 4, 8, 16, 32, 64):
        run = run + pltpu.roll(run, width - step, 1)
    windowed = pltpu.roll(run, SMOOTH, 1) + pltpu.roll(padded, width - SMOOTH, 1)
    windowed = windowed[:, LANES : LANES + FREQS]

    row = lax.broadcasted_iota(jnp.int32, (ROWS, LANES), 0)
    offsets = jnp.zeros((ROWS, LANES), jnp.int32)
    alive = jnp.zeros((ROWS, LANES), jnp.int32)
    for k in range(SEGS):
        for c in range(CH):
            offsets = jnp.where(row == k * CH + c, info_ref[1 + k, c], offsets)
            alive = jnp.where(row == k * CH + c, info_ref[3, c], alive)
    alive = alive.astype(jnp.float32)
    lane = lax.broadcasted_iota(jnp.int32, (ROWS, LANES), 1)
    head = windowed[:, :LANES] / (jnp.minimum(lane, SMOOTH) + (SMOOTH + 1)).astype(jnp.float32)
    tail = windowed[:, FREQS - LANES :] / (
        jnp.minimum(LANES - 1 - lane, SMOOTH) + (SMOOTH + 1)
    ).astype(jnp.float32)
    middle = windowed[:, LANES : FREQS - LANES] * (1.0 / (2 * SMOOTH + 1))
    smoothed = jnp.concatenate([head, middle, tail], axis=1) + EPSILON
    scale = jnp.concatenate([alive] * (FREQS // LANES), axis=1) / smoothed

    inner = unit_circle(((lane + 1) * offsets) & (NSAMP - 1))
    groups = [inner]
    for j in (1, 2, 3):
        groups.append(turned(inner, unit_circle((j * LANES * offsets) & (NSAMP - 1))))
    angles = list(groups)
    for j in range(1, FREQS // (4 * LANES)):
        outer = unit_circle((j * 4 * LANES * offsets) & (NSAMP - 1))
        angles += [turned(group, outer) for group in groups]
    cosine = jnp.concatenate([pair[0] for pair in angles], axis=1)
    sine = jnp.concatenate([pair[1] for pair in angles], axis=1)
    white = [
        ((real * cosine - imag * sine) * scale).astype(jnp.bfloat16).astype(jnp.float32),
        ((real * sine + imag * cosine) * scale).astype(jnp.bfloat16).astype(jnp.float32),
    ]
    for q in range(2):
        for i in range(2):
            keep_ref[i, q, 0:ROWS] = white[q][:, i * SHARE : (i + 1) * SHARE]
        scaled = white[q] * (1.0 / math.sqrt(SEGS))
        for i in range(FREQS // SLICE):
            chan_ref[i, q] = scaled[:, i * SLICE : (i + 1) * SLICE]

    code = jnp.int32(0)
    for group, line in enumerate(NEAR):
        packed = sum((int(to) // 2 % 2) << n for n, to in enumerate(line))
        code = jnp.where(block // 8 == group, packed, code)
    upper = (code >> place) & 1
    picked = []
    for q in range(2):
        for k in range(SEGS):
            for r in range(SG):
                at = info_ref[0, block * SG + r] - block * CH + k * CH
                picked.append(keep_ref[upper, q, pl.ds(at, 1), :])
    src_ref[...] = jnp.concatenate(picked, axis=0).astype(jnp.bfloat16)


INNER = 64


HALF = LAGS // 2
PAIRS = 2 * CH * 16


def table_kernel(after_ref, table_ref, inner_ref, outer_ref):
    lane = lax.broadcasted_iota(jnp.int32, (INNER, LAGS), 1)
    lags = jnp.where(lane < HALF, lane, lane - (HALF - 1))
    row = lax.broadcasted_iota(jnp.int32, (INNER, LAGS), 0)
    inner_ref[0], inner_ref[1] = unit_circle(((row + 1) * lags) & (NSAMP - 1))
    for q, values in enumerate(unit_circle((row * INNER * lags) & (NSAMP - 1))):
        for block in range(LAGS // LANES):
            outer_ref[q, block] = values[:, block * LANES : (block + 1) * LANES]
    for block in range(LAGS // LANES):
        lanes = slice(block * LANES, (block + 1) * LANES)
        for i in range(INNER // 16):
            rows = slice(i * 16, i * 16 + 16)
            icos, isin = inner_ref[0, rows, lanes], inner_ref[1, rows, lanes]

            def put(at, carry, icos=icos, isin=isin, block=block, lanes=lanes, i=i):
                wcos = jnp.broadcast_to(outer_ref[0, block, pl.ds(at, 1), :], (16, LANES))
                wsin = jnp.broadcast_to(outer_ref[1, block, pl.ds(at, 1), :], (16, LANES))
                if lanes.start < HALF:
                    value = icos * wcos - isin * wsin
                else:
                    value = isin * wcos + icos * wsin
                table_ref[at, i * 16 : i * 16 + 16, lanes] = value.astype(jnp.bfloat16)
                return carry

            lax.fori_loop(0, FREQS // INNER, put, 0, unroll=16)


def correlate_kernel(
    core_ref, mine_ref, other_ref, chan_ref, table_ref, out_ref,
    even_cross, odd_cross, cos_sum, sin_sum, last_sum, sum_ref
):
    low = lax.broadcasted_iota(jnp.int32, (8, LANES), 0) < 4

    def cross(step, cross_ref):
        upper, part = divmod(step, SHARE // SLICE)
        for block in range(SLICE // LANES):
            lanes = slice(block * LANES, (block + 1) * LANES)
            from_lanes = slice(part * SLICE + block * LANES, part * SLICE + (block + 1) * LANES)
            for half, src_ref in enumerate((mine_ref, other_ref)):
                tiles = []
                for x in (0, 2):
                    first = src_ref[upper, x, :, from_lanes].astype(jnp.float32)
                    second = src_ref[upper, x + 1, :, from_lanes].astype(jnp.float32)
                    parts = []
                    for q in range(2):
                        one, two = first[q * 8 : q * 8 + 8], second[q * 8 : q * 8 + 8]
                        parts.append(jnp.where(low, one, pltpu.roll(two, 4, 0)))
                        parts.append(jnp.where(low, pltpu.roll(one, 4, 0), two))
                    tiles.append(parts)
                for c in range(CH):
                    creal, cimag = [
                        [
                            jnp.broadcast_to(
                                chan_ref[step, q, k * CH + c : k * CH + c + 1, lanes],
                                (8, LANES),
                            )
                            for k in range(SEGS)
                        ]
                        for q in range(2)
                    ]
                    reals, imags = [], []
                    for real0, real1, imag0, imag1 in tiles:
                        reals.append(
                            (creal[0] * real0 + cimag[0] * imag0) + (creal[1] * real1 + cimag[1] * imag1)
                        )
                        imags.append(
                            (cimag[0] * real0 - creal[0] * imag0) + (cimag[1] * real1 - creal[1] * imag1)
                        )
                    at = half * CH * 16 + c * 16
                    for q, got in enumerate((reals, imags)):
                        rows = jnp.concatenate(got, axis=0).astype(jnp.bfloat16)
                        cross_ref[q, at : at + 16, lanes] = rows
                        if q == 0:
                            last_sum[at : at + 16] += rows.astype(jnp.float32)

    def add(step, cross_ref):
        chunk = table_ref[pl.ds(step * (SLICE // INNER), SLICE // INNER)].reshape(SLICE, LAGS)
        cos_sum[...] += jnp.dot(cross_ref[0], chunk[:, :HALF], preferred_element_type=jnp.float32)
        sin_sum[...] += jnp.dot(cross_ref[1], chunk[:, HALF:], preferred_element_type=jnp.float32)

    cos_sum[...] = jnp.zeros_like(cos_sum)
    sin_sum[...] = jnp.zeros_like(sin_sum)
    last_sum[...] = jnp.zeros_like(last_sum)
    steps = FREQS // SLICE
    buffers = (even_cross, odd_cross)
    cross(0, even_cross)
    for step in range(1, steps):
        cross(step, buffers[step % 2])
        add(step - 1, buffers[(step - 1) % 2])
    add(steps - 1, buffers[(steps - 1) % 2])

    period = lax.broadcasted_iota(jnp.int32, (8, LANES), 1) + 1
    wave = unit_circle((period * HALF) & (NSAMP - 1))[0].astype(jnp.bfloat16).astype(jnp.float32)
    cos_last = jnp.sum(last_sum[...] * wave[0:1], axis=1, keepdims=True)
    cosines, sines = cos_sum[...], sin_sum[...]
    lane = lax.broadcasted_iota(jnp.int32, (PAIRS, HALF), 1)
    positive = cosines - jnp.where(lane == 0, 0.0, pltpu.roll(sines, 1, 1))
    negative = jnp.where(lane == HALF - 1, cos_last, pltpu.roll(cosines, HALF - 1, 1)) + sines
    first = negative.astype(jnp.bfloat16)
    rest = negative - first.astype(jnp.float32)
    second = rest.astype(jnp.bfloat16)
    third = (rest - second.astype(jnp.float32)).astype(jnp.bfloat16)
    mirror = (
        lax.broadcasted_iota(jnp.int32, (HALF, HALF), 0) + lax.broadcasted_iota(jnp.int32, (HALF, HALF), 1)
        == HALF - 1
    ).astype(jnp.float32).astype(jnp.bfloat16)
    flipped = [jnp.dot(t, mirror, preferred_element_type=jnp.float32) for t in (first, second, third)]
    factor = 1.0 / math.sqrt(FREQS)
    sum_ref[:, :, :, :HALF] = ((flipped[0] + flipped[1] + flipped[2]) * factor).reshape(2, CH, 16, HALF)
    sum_ref[:, :, :, HALF:] = (positive * factor).reshape(2, CH, 16, HALF)

    core = core_ref[0]
    for c in range(CH):
        zero, one = sum_ref[core, c], sum_ref[1 - core, c]
        for x in range(4):
            rows = slice(x * 4, x * 4 + 4)
            out_ref[c, x * 8 : x * 8 + 8, :] = jnp.concatenate([zero[rows], one[rows]], axis=0)


def scattered():
    pairs = []
    for group in range(8):
        for n in range(8):
            pairs.append((group * 8 + n, int(NEAR[group][n]) * 8 + group))
    return pairs


def body(spectra, dead_mask, seg_offsets, src_index):
    pos = {axis: lax.axis_index(axis).astype(jnp.int32) for axis in ("u", "v", "h", "x", "c", "n")}
    wide_pos = (((pos["u"] * 2 + pos["v"]) * 2 + pos["h"]) * 4 + pos["x"]) * 2 + pos["c"]
    rows = jnp.transpose(spectra, (2, 1, 0, 3)).reshape(2 * ROWS, SLICE)
    width = src_index.shape[0]
    info = jnp.concatenate(
        [
            src_index[None],
            jnp.pad(seg_offsets.T, ((0, 0), (0, width - CH))),
            jnp.pad(dead_mask, (0, width - CH))[None],
            jnp.pad(jnp.stack([wide_pos, pos["n"]]), (0, width - 2))[None],
        ]
    )
    pieces = lax.all_to_all(jnp.broadcast_to(rows[None], (8, 2 * ROWS, SLICE)), "n", 0, 0)

    vmem = pl.BlockSpec(memory_space=pltpu.VMEM)
    smem = pl.BlockSpec(memory_space=pltpu.SMEM)
    chan, src_out = pl.pallas_call(
        whiten_kernel,
        out_shape=(
            jax.ShapeDtypeStruct((FREQS // SLICE, 2, ROWS, SLICE), jnp.float32),
            jax.ShapeDtypeStruct((16, SHARE), jnp.bfloat16),
        ),
        in_specs=[smem, vmem],
        out_specs=(vmem, vmem),
        scratch_shapes=[pltpu.VMEM((2, 2, 16, SHARE), jnp.float32)],
        compiler_params=pltpu.CompilerParams(vmem_limit_bytes=32 * 2**20),
        name="whiten",
    )(info, pieces)

    moved = lax.ppermute(src_out, ("u", "v", "h", "n"), scattered())
    mine = lax.all_to_all(jnp.broadcast_to(moved[None], (8,) + moved.shape), ("v", "x"), 0, 0)
    mine = mine.reshape((2, 4) + moved.shape)
    other = lax.ppermute(mine, "c", [(0, 1), (1, 0)])

    table = pl.pallas_call(
        table_kernel,
        in_specs=[pl.BlockSpec(memory_space=pl.ANY)],
        out_specs=vmem,
        scratch_shapes=[
            pltpu.VMEM((2, INNER, LAGS), jnp.float32),
            pltpu.VMEM((2, LAGS // LANES, FREQS // INNER, LANES), jnp.float32),
        ],
        out_shape=jax.ShapeDtypeStruct((FREQS // INNER, INNER, LAGS), jnp.bfloat16),
        compiler_params=pltpu.CompilerParams(vmem_limit_bytes=16 * 2**20),
        cost_estimate=pl.CostEstimate(flops=4 * FREQS * LAGS, bytes_accessed=2 * FREQS * LAGS, transcendentals=0),
        name="lag_table",
    )(mine)

    out = pl.pallas_call(
        correlate_kernel,
        in_specs=[smem, vmem, vmem, vmem, vmem],
        out_specs=vmem,
        scratch_shapes=[
            pltpu.VMEM((2, PAIRS, SLICE), jnp.bfloat16),
            pltpu.VMEM((2, PAIRS, SLICE), jnp.bfloat16),
            pltpu.VMEM((PAIRS, HALF), jnp.float32),
            pltpu.VMEM((PAIRS, HALF), jnp.float32),
            pltpu.VMEM((PAIRS, LANES), jnp.float32),
            pltpu.VMEM((2, CH, 16, LAGS), jnp.float32),
        ],
        out_shape=jax.ShapeDtypeStruct((CH, 32, LAGS), jnp.float32),
        compiler_params=pltpu.CompilerParams(vmem_limit_bytes=20 * 2**20),
        name="correlate",
    )(pos["c"].reshape(1), mine, other, chan, table)
    return jnp.transpose(out, (1, 0, 2))


def solution(mesh):
    parts = Mesh(mesh.devices.reshape(2, 2, 2, 4, 2, 8), ("u", "v", "h", "x", "c", "n"))
    wide = ("u", "v", "h", "x", "c")
    placed = (P(wide, None, None, "n"), P(wide), P(wide, None), P())
    return jax.shard_map(
        body, mesh=parts, in_specs=placed, out_specs=P("n", wide, None), check_vma=False
    )
```

```python
import math

import jax
import jax.numpy as jnp
from jax import lax
from jax.experimental import pallas as pl
from jax.experimental.pallas import tpu as pltpu
from jax.sharding import Mesh, PartitionSpec as P

NSAMP = 32768
LAGS = 512
SMOOTH = 64
EPSILON = 1e-06
FREQS = 4096
SLICE = 512
CH = 6
ROWS = 12
SG = 4
SEGS = 2
LANES = 128
SHARE = FREQS // 2


def unit_circle(residue):
    quarter = NSAMP // 4
    quadrant = (residue + quarter // 2) >> 13
    rest = (residue - quadrant * quarter).astype(jnp.float32) * (2.0 * math.pi / NSAMP)
    sq = rest * rest
    sine = rest * (1.0 + sq * (-1.0 / 6 + sq * (1.0 / 120 + sq * (-1.0 / 5040))))
    cosine = 1.0 + sq * (-0.5 + sq * (1.0 / 24 + sq * (-1.0 / 720 + sq * (1.0 / 40320))))
    swap = (quadrant & 1) == 1
    first = jnp.where(swap, sine, cosine)
    second = jnp.where(swap, cosine, sine)
    first = jnp.where(((quadrant + 1) & 2) == 2, -first, first)
    second = jnp.where((quadrant & 2) == 2, -second, second)
    return first, second


def turned(pair, by):
    return pair[0] * by[0] - pair[1] * by[1], pair[1] * by[0] + pair[0] * by[1]


NEAR = ("42601375", "35710264", "20643157", "02175346", "13420657", "02643175", "31576024", "20467153")


def whiten_kernel(info_ref, pieces_ref, chan_ref, src_ref, keep_ref):
    block, place = info_ref[4, 0], info_ref[4, 1]
    far = place // 4
    slices = [pieces_ref[p, (m + far) % 2] for m in range(2) for p in range(4)]
    cells = jnp.concatenate(slices, axis=1).astype(jnp.float32)
    real, imag = cells[0:ROWS], cells[ROWS : 2 * ROWS]
    amplitude = jnp.sqrt(real * real + imag * imag)
    edge = jnp.zeros((ROWS, LANES), jnp.float32)
    padded = jnp.concatenate([edge, amplitude, edge], axis=1)
    width = FREQS + 2 * LANES
    run = padded
    for step in (1, 2, 4, 8, 16, 32, 64):
        run = run + pltpu.roll(run, width - step, 1)
    windowed = pltpu.roll(run, SMOOTH, 1) + pltpu.roll(padded, width - SMOOTH, 1)
    windowed = windowed[:, LANES : LANES + FREQS]

    row = lax.broadcasted_iota(jnp.int32, (ROWS, LANES), 0)
    offsets = jnp.zeros((ROWS, LANES), jnp.int32)
    alive = jnp.zeros((ROWS, LANES), jnp.int32)
    for k in range(SEGS):
        for c in range(CH):
            offsets = jnp.where(row == k * CH + c, info_ref[1 + k, c], offsets)
            alive = jnp.where(row == k * CH + c, info_ref[3, c], alive)
    alive = alive.astype(jnp.float32)
    lane = lax.broadcasted_iota(jnp.int32, (ROWS, LANES), 1)
    head = windowed[:, :LANES] / (jnp.minimum(lane, SMOOTH) + (SMOOTH + 1)).astype(jnp.float32)
    tail = windowed[:, FREQS - LANES :] / (
        jnp.minimum(LANES - 1 - lane, SMOOTH) + (SMOOTH + 1)
    ).astype(jnp.float32)
    middle = windowed[:, LANES : FREQS - LANES] * (1.0 / (2 * SMOOTH + 1))
    smoothed = jnp.concatenate([head, middle, tail], axis=1) + EPSILON
    scale = jnp.concatenate([alive] * (FREQS // LANES), axis=1) / smoothed

    inner = unit_circle(((lane + 1) * offsets) & (NSAMP - 1))
    groups = [inner]
    for j in (1, 2, 3):
        groups.append(turned(inner, unit_circle((j * LANES * offsets) & (NSAMP - 1))))
    angles = list(groups)
    for j in range(1, FREQS // (4 * LANES)):
        outer = unit_circle((j * 4 * LANES * offsets) & (NSAMP - 1))
        angles += [turned(group, outer) for group in groups]
    cosine = jnp.concatenate([pair[0] for pair in angles], axis=1)
    sine = jnp.concatenate([pair[1] for pair in angles], axis=1)
    white = [
        ((real * cosine - imag * sine) * scale).astype(jnp.bfloat16).astype(jnp.float32),
        ((real * sine + imag * cosine) * scale).astype(jnp.bfloat16).astype(jnp.float32),
    ]
    for q in range(2):
        for i in range(2):
            keep_ref[i, q, 0:ROWS] = white[q][:, i * SHARE : (i + 1) * SHARE]
        scaled = white[q] * (1.0 / math.sqrt(SEGS))
        for i in range(FREQS // SLICE):
            chan_ref[i, q] = scaled[:, i * SLICE : (i + 1) * SLICE]

    code = jnp.int32(0)
    for group, line in enumerate(NEAR):
        packed = sum((int(to) // 2 % 2) << n for n, to in enumerate(line))
        code = jnp.where(block // 8 == group, packed, code)
    upper = (code >> place) & 1
    picked = []
    for q in range(2):
        for k in range(SEGS):
            for r in range(SG):
                at = info_ref[0, block * SG + r] - block * CH + k * CH
                picked.append(keep_ref[upper, q, pl.ds(at, 1), :])
    src_ref[...] = jnp.concatenate(picked, axis=0).astype(jnp.bfloat16)


INNER = 64


HALF = LAGS // 2
PAIRS = 2 * CH * 16


def table_kernel(after_ref, table_ref, inner_ref, outer_ref):
    lane = lax.broadcasted_iota(jnp.int32, (INNER, LAGS), 1)
    lags = jnp.where(lane < HALF, lane, lane - (HALF - 1))
    row = lax.broadcasted_iota(jnp.int32, (INNER, LAGS), 0)
    inner_ref[0], inner_ref[1] = unit_circle(((row + 1) * lags) & (NSAMP - 1))
    for q, values in enumerate(unit_circle((row * INNER * lags) & (NSAMP - 1))):
        for block in range(LAGS // LANES):
            outer_ref[q, block] = values[:, block * LANES : (block + 1) * LANES]
    for block in range(LAGS // LANES):
        lanes = slice(block * LANES, (block + 1) * LANES)
        for i in range(INNER // 16):
            rows = slice(i * 16, i * 16 + 16)
            icos, isin = inner_ref[0, rows, lanes], inner_ref[1, rows, lanes]

            def put(at, carry, icos=icos, isin=isin, block=block, lanes=lanes, i=i):
                wcos = jnp.broadcast_to(outer_ref[0, block, pl.ds(at, 1), :], (16, LANES))
                wsin = jnp.broadcast_to(outer_ref[1, block, pl.ds(at, 1), :], (16, LANES))
                if lanes.start < HALF:
                    value = icos * wcos - isin * wsin
                else:
                    value = isin * wcos + icos * wsin
                table_ref[at, i * 16 : i * 16 + 16, lanes] = value.astype(jnp.bfloat16)
                return carry

            lax.fori_loop(0, FREQS // INNER, put, 0, unroll=16)


def correlate_kernel(
    core_ref, mine_ref, other_ref, chan_ref, table_ref, out_ref,
    even_cross, odd_cross, cos_sum, sin_sum, last_sum, sum_ref
):
    low = lax.broadcasted_iota(jnp.int32, (8, LANES), 0) < 4

    def cross(step, cross_ref):
        upper, part = divmod(step, SHARE // SLICE)
        for block in range(SLICE // LANES):
            lanes = slice(block * LANES, (block + 1) * LANES)
            from_lanes = slice(part * SLICE + block * LANES, part * SLICE + (block + 1) * LANES)
            for half, src_ref in enumerate((mine_ref, other_ref)):
                tiles = []
                for x in (0, 2):
                    first = src_ref[upper, x, :, from_lanes].astype(jnp.float32)
                    second = src_ref[upper, x + 1, :, from_lanes].astype(jnp.float32)
                    parts = []
                    for q in range(2):
                        one, two = first[q * 8 : q * 8 + 8], second[q * 8 : q * 8 + 8]
                        parts.append(jnp.where(low, one, pltpu.roll(two, 4, 0)))
                        parts.append(jnp.where(low, pltpu.roll(one, 4, 0), two))
                    tiles.append(parts)
                for c in range(CH):
                    creal, cimag = [
                        [
                            jnp.broadcast_to(
                                chan_ref[step, q, k * CH + c : k * CH + c + 1, lanes],
                                (8, LANES),
                            )
                            for k in range(SEGS)
                        ]
                        for q in range(2)
                    ]
                    reals, imags = [], []
                    for real0, real1, imag0, imag1 in tiles:
                        reals.append(
                            (creal[0] * real0 + cimag[0] * imag0) + (creal[1] * real1 + cimag[1] * imag1)
                        )
                        imags.append(
                            (cimag[0] * real0 - creal[0] * imag0) + (cimag[1] * real1 - creal[1] * imag1)
                        )
                    at = half * CH * 16 + c * 16
                    for q, got in enumerate((reals, imags)):
                        rows = jnp.concatenate(got, axis=0).astype(jnp.bfloat16)
                        cross_ref[q, at : at + 16, lanes] = rows
                        if q == 0:
                            last_sum[at : at + 16] += rows.astype(jnp.float32)

    def add(step, cross_ref):
        chunk = table_ref[pl.ds(step * (SLICE // INNER), SLICE // INNER)].reshape(SLICE, LAGS)
        cos_sum[...] += jnp.dot(cross_ref[0], chunk[:, :HALF], preferred_element_type=jnp.float32)
        sin_sum[...] += jnp.dot(cross_ref[1], chunk[:, HALF:], preferred_element_type=jnp.float32)

    cos_sum[...] = jnp.zeros_like(cos_sum)
    sin_sum[...] = jnp.zeros_like(sin_sum)
    last_sum[...] = jnp.zeros_like(last_sum)
    steps = FREQS // SLICE
    buffers = (even_cross, odd_cross)
    cross(0, even_cross)
    for step in range(1, steps):
        cross(step, buffers[step % 2])
        add(step - 1, buffers[(step - 1) % 2])
    add(steps - 1, buffers[(steps - 1) % 2])

    period = lax.broadcasted_iota(jnp.int32, (8, LANES), 1) + 1
    wave = unit_circle((period * HALF) & (NSAMP - 1))[0].astype(jnp.bfloat16).astype(jnp.float32)
    cos_last = jnp.sum(last_sum[...] * wave[0:1], axis=1, keepdims=True)
    cosines, sines = cos_sum[...], sin_sum[...]
    lane = lax.broadcasted_iota(jnp.int32, (PAIRS, HALF), 1)
    positive = cosines - jnp.where(lane == 0, 0.0, pltpu.roll(sines, 1, 1))
    negative = jnp.where(lane == HALF - 1, cos_last, pltpu.roll(cosines, HALF - 1, 1)) + sines
    first = negative.astype(jnp.bfloat16)
    rest = negative - first.astype(jnp.float32)
    second = rest.astype(jnp.bfloat16)
    third = (rest - second.astype(jnp.float32)).astype(jnp.bfloat16)
    mirror = (
        lax.broadcasted_iota(jnp.int32, (HALF, HALF), 0) + lax.broadcasted_iota(jnp.int32, (HALF, HALF), 1)
        == HALF - 1
    ).astype(jnp.float32).astype(jnp.bfloat16)
    flipped = [jnp.dot(t, mirror, preferred_element_type=jnp.float32) for t in (first, second, third)]
    factor = 1.0 / math.sqrt(FREQS)
    sum_ref[:, :, :, :HALF] = ((flipped[0] + flipped[1] + flipped[2]) * factor).reshape(2, CH, 16, HALF)
    sum_ref[:, :, :, HALF:] = (positive * factor).reshape(2, CH, 16, HALF)

    core = core_ref[0]
    for c in range(CH):
        zero, one = sum_ref[core, c], sum_ref[1 - core, c]
        for x in range(4):
            rows = slice(x * 4, x * 4 + 4)
            out_ref[c, x * 8 : x * 8 + 8, :] = jnp.concatenate([zero[rows], one[rows]], axis=0)


def scattered():
    pairs = []
    for group in range(8):
        for n in range(8):
            pairs.append((group * 8 + n, int(NEAR[group][n]) * 8 + group))
    return pairs


def body(spectra, dead_mask, seg_offsets, src_index):
    pos = {axis: lax.axis_index(axis).astype(jnp.int32) for axis in ("u", "v", "h", "x", "c", "m", "p")}
    wide_pos = (((pos["u"] * 2 + pos["v"]) * 2 + pos["h"]) * 4 + pos["x"]) * 2 + pos["c"]
    rows = jnp.transpose(spectra, (2, 1, 0, 3)).reshape(2 * ROWS, SLICE)
    width = src_index.shape[0]
    info = jnp.concatenate(
        [
            src_index[None],
            jnp.pad(seg_offsets.T, ((0, 0), (0, width - CH))),
            jnp.pad(dead_mask, (0, width - CH))[None],
            jnp.pad(jnp.stack([wide_pos, pos["m"] * 4 + pos["p"]]), (0, width - 2))[None],
        ]
    )
    pair = jnp.stack([rows, lax.ppermute(rows, "m", [(0, 1), (1, 0)])])
    pieces = lax.all_to_all(jnp.broadcast_to(pair[None], (4,) + pair.shape), "p", 0, 0)

    vmem = pl.BlockSpec(memory_space=pltpu.VMEM)
    smem = pl.BlockSpec(memory_space=pltpu.SMEM)
    chan, src_out = pl.pallas_call(
        whiten_kernel,
        out_shape=(
            jax.ShapeDtypeStruct((FREQS // SLICE, 2, ROWS, SLICE), jnp.float32),
            jax.ShapeDtypeStruct((16, SHARE), jnp.bfloat16),
        ),
        in_specs=[smem, vmem],
        out_specs=(vmem, vmem),
        scratch_shapes=[pltpu.VMEM((2, 2, 16, SHARE), jnp.float32)],
        compiler_params=pltpu.CompilerParams(vmem_limit_bytes=32 * 2**20),
        name="whiten",
    )(info, pieces)

    moved = lax.ppermute(src_out, ("u", "v", "h", "m", "p"), scattered())
    mine = lax.all_to_all(jnp.broadcast_to(moved[None], (8,) + moved.shape), ("v", "x"), 0, 0)
    mine = mine.reshape((2, 4) + moved.shape)
    other = lax.ppermute(mine, "c", [(0, 1), (1, 0)])

    table = pl.pallas_call(
        table_kernel,
        in_specs=[pl.BlockSpec(memory_space=pl.ANY)],
        out_specs=vmem,
        scratch_shapes=[
            pltpu.VMEM((2, INNER, LAGS), jnp.float32),
            pltpu.VMEM((2, LAGS // LANES, FREQS // INNER, LANES), jnp.float32),
        ],
        out_shape=jax.ShapeDtypeStruct((FREQS // INNER, INNER, LAGS), jnp.bfloat16),
        compiler_params=pltpu.CompilerParams(vmem_limit_bytes=16 * 2**20),
        cost_estimate=pl.CostEstimate(flops=4 * FREQS * LAGS, bytes_accessed=2 * FREQS * LAGS, transcendentals=0),
        name="lag_table",
    )(mine)

    out = pl.pallas_call(
        correlate_kernel,
        in_specs=[smem, vmem, vmem, vmem, vmem],
        out_specs=vmem,
        scratch_shapes=[
            pltpu.VMEM((2, PAIRS, SLICE), jnp.bfloat16),
            pltpu.VMEM((2, PAIRS, SLICE), jnp.bfloat16),
            pltpu.VMEM((PAIRS, HALF), jnp.float32),
            pltpu.VMEM((PAIRS, HALF), jnp.float32),
            pltpu.VMEM((PAIRS, LANES), jnp.float32),
            pltpu.VMEM((2, CH, 16, LAGS), jnp.float32),
        ],
        out_shape=jax.ShapeDtypeStruct((CH, 32, LAGS), jnp.float32),
        compiler_params=pltpu.CompilerParams(vmem_limit_bytes=20 * 2**20),
        name="correlate",
    )(pos["c"].reshape(1), mine, other, chan, table)
    return jnp.transpose(out, (1, 0, 2))


def solution(mesh):
    parts = Mesh(mesh.devices.reshape(2, 2, 2, 4, 2, 2, 4), ("u", "v", "h", "x", "c", "m", "p"))
    line = ("m", "p")
    wide = ("u", "v", "h", "x", "c")
    placed = (P(wide, None, None, line), P(wide), P(wide, None), P())
    return jax.shard_map(
        body, mesh=parts, in_specs=placed, out_specs=P(line, wide, None), check_vma=False
    )
```

```python
import math

import jax
import jax.numpy as jnp
from jax import lax
from jax.experimental import pallas as pl
from jax.experimental.pallas import tpu as pltpu
from jax.sharding import Mesh, PartitionSpec as P

NSAMP = 32768
LAGS = 512
SMOOTH = 64
EPSILON = 1e-06
FREQS = 4096
SLICE = 512
CH = 6
ROWS = 12
SG = 4
SEGS = 2
LANES = 128
SHARE = FREQS // 2


def unit_circle(residue):
    quarter = NSAMP // 4
    quadrant = (residue + quarter // 2) >> 13
    rest = (residue - quadrant * quarter).astype(jnp.float32) * (2.0 * math.pi / NSAMP)
    sq = rest * rest
    sine = rest * (1.0 + sq * (-1.0 / 6 + sq * (1.0 / 120 + sq * (-1.0 / 5040))))
    cosine = 1.0 + sq * (-0.5 + sq * (1.0 / 24 + sq * (-1.0 / 720 + sq * (1.0 / 40320))))
    swap = (quadrant & 1) == 1
    first = jnp.where(swap, sine, cosine)
    second = jnp.where(swap, cosine, sine)
    first = jnp.where(((quadrant + 1) & 2) == 2, -first, first)
    second = jnp.where((quadrant & 2) == 2, -second, second)
    return first, second


def turned(pair, by):
    return pair[0] * by[0] - pair[1] * by[1], pair[1] * by[0] + pair[0] * by[1]


NEAR = ("42601375", "35710264", "20643157", "02175346", "13420657", "02643175", "31576024", "20467153")


def whiten_kernel(info_ref, pieces_ref, chan_ref, src_ref, keep_ref):
    block, place = info_ref[4, 0], info_ref[4, 1]
    far = place // 4
    slices = [pieces_ref[p, (m + far) % 2] for m in range(2) for p in range(4)]
    cells = jnp.concatenate(slices, axis=1).astype(jnp.float32)
    real, imag = cells[0:ROWS], cells[ROWS : 2 * ROWS]
    amplitude = jnp.sqrt(real * real + imag * imag)
    edge = jnp.zeros((ROWS, LANES), jnp.float32)
    padded = jnp.concatenate([edge, amplitude, edge], axis=1)
    width = FREQS + 2 * LANES
    run = padded
    for step in (1, 2, 4, 8, 16, 32, 64):
        run = run + pltpu.roll(run, width - step, 1)
    windowed = pltpu.roll(run, SMOOTH, 1) + pltpu.roll(padded, width - SMOOTH, 1)
    windowed = windowed[:, LANES : LANES + FREQS]

    row = lax.broadcasted_iota(jnp.int32, (ROWS, LANES), 0)
    offsets = jnp.zeros((ROWS, LANES), jnp.int32)
    alive = jnp.zeros((ROWS, LANES), jnp.int32)
    for k in range(SEGS):
        for c in range(CH):
            offsets = jnp.where(row == k * CH + c, info_ref[1 + k, c], offsets)
            alive = jnp.where(row == k * CH + c, info_ref[3, c], alive)
    alive = alive.astype(jnp.float32)
    lane = lax.broadcasted_iota(jnp.int32, (ROWS, LANES), 1)
    head = windowed[:, :LANES] / (jnp.minimum(lane, SMOOTH) + (SMOOTH + 1)).astype(jnp.float32)
    tail = windowed[:, FREQS - LANES :] / (
        jnp.minimum(LANES - 1 - lane, SMOOTH) + (SMOOTH + 1)
    ).astype(jnp.float32)
    middle = windowed[:, LANES : FREQS - LANES] * (1.0 / (2 * SMOOTH + 1))
    smoothed = jnp.concatenate([head, middle, tail], axis=1) + EPSILON
    scale = jnp.concatenate([alive] * (FREQS // LANES), axis=1) / smoothed

    inner = unit_circle(((lane + 1) * offsets) & (NSAMP - 1))
    groups = [inner]
    for j in (1, 2, 3):
        groups.append(turned(inner, unit_circle((j * LANES * offsets) & (NSAMP - 1))))
    angles = list(groups)
    for j in range(1, FREQS // (4 * LANES)):
        outer = unit_circle((j * 4 * LANES * offsets) & (NSAMP - 1))
        angles += [turned(group, outer) for group in groups]
    cosine = jnp.concatenate([pair[0] for pair in angles], axis=1)
    sine = jnp.concatenate([pair[1] for pair in angles], axis=1)
    white = [
        ((real * cosine - imag * sine) * scale).astype(jnp.bfloat16).astype(jnp.float32),
        ((real * sine + imag * cosine) * scale).astype(jnp.bfloat16).astype(jnp.float32),
    ]
    for q in range(2):
        for i in range(2):
            keep_ref[i, q, 0:ROWS] = white[q][:, i * SHARE : (i + 1) * SHARE]
        scaled = white[q] * (1.0 / math.sqrt(SEGS))
        for i in range(FREQS // SLICE):
            chan_ref[i, q] = scaled[:, i * SLICE : (i + 1) * SLICE]

    code = jnp.int32(0)
    for group, line in enumerate(NEAR):
        packed = sum((int(to) // 2 % 2) << n for n, to in enumerate(line))
        code = jnp.where(block // 8 == group, packed, code)
    upper = (code >> place) & 1
    picked = []
    for q in range(2):
        for k in range(SEGS):
            for r in range(SG):
                at = info_ref[0, block * SG + r] - block * CH + k * CH
                picked.append(keep_ref[upper, q, pl.ds(at, 1), :])
    src_ref[...] = jnp.concatenate(picked, axis=0).astype(jnp.bfloat16)


INNER = 64


HALF = LAGS // 2
PAIRS = 2 * CH * 16


def table_kernel(after_ref, table_ref, inner_ref, outer_ref):
    lane = lax.broadcasted_iota(jnp.int32, (INNER, LAGS), 1)
    lags = jnp.where(lane < HALF, lane, lane - (HALF - 1))
    row = lax.broadcasted_iota(jnp.int32, (INNER, LAGS), 0)
    inner_ref[0], inner_ref[1] = unit_circle(((row + 1) * lags) & (NSAMP - 1))
    for q, values in enumerate(unit_circle((row * INNER * lags) & (NSAMP - 1))):
        for block in range(LAGS // LANES):
            outer_ref[q, block] = values[:, block * LANES : (block + 1) * LANES]
    for block in range(LAGS // LANES):
        lanes = slice(block * LANES, (block + 1) * LANES)
        for i in range(INNER // 16):
            rows = slice(i * 16, i * 16 + 16)
            icos, isin = inner_ref[0, rows, lanes], inner_ref[1, rows, lanes]

            def put(at, carry, icos=icos, isin=isin, block=block, lanes=lanes, i=i):
                wcos = jnp.broadcast_to(outer_ref[0, block, pl.ds(at, 1), :], (16, LANES))
                wsin = jnp.broadcast_to(outer_ref[1, block, pl.ds(at, 1), :], (16, LANES))
                if lanes.start < HALF:
                    value = icos * wcos - isin * wsin
                else:
                    value = isin * wcos + icos * wsin
                table_ref[at, i * 16 : i * 16 + 16, lanes] = value.astype(jnp.bfloat16)
                return carry

            lax.fori_loop(0, FREQS // INNER, put, 0, unroll=16)


def correlate_kernel(
    core_ref, mine_ref, other_ref, chan_ref, table_ref, out_ref,
    even_cross, odd_cross, cos_sum, sin_sum, last_sum, sum_ref
):
    low = lax.broadcasted_iota(jnp.int32, (8, LANES), 0) < 4

    def cross(step, cross_ref):
        upper, part = divmod(step, SHARE // SLICE)
        for block in range(SLICE // LANES):
            lanes = slice(block * LANES, (block + 1) * LANES)
            from_lanes = slice(part * SLICE + block * LANES, part * SLICE + (block + 1) * LANES)
            for half, src_ref in enumerate((mine_ref, other_ref)):
                tiles = []
                for x in (0, 2):
                    first = src_ref[upper, x, :, from_lanes].astype(jnp.float32)
                    second = src_ref[upper, x + 1, :, from_lanes].astype(jnp.float32)
                    parts = []
                    for q in range(2):
                        one, two = first[q * 8 : q * 8 + 8], second[q * 8 : q * 8 + 8]
                        parts.append(jnp.where(low, one, pltpu.roll(two, 4, 0)))
                        parts.append(jnp.where(low, pltpu.roll(one, 4, 0), two))
                    tiles.append(parts)
                for c in range(CH):
                    creal, cimag = [
                        [
                            jnp.broadcast_to(
                                chan_ref[step, q, k * CH + c : k * CH + c + 1, lanes],
                                (8, LANES),
                            )
                            for k in range(SEGS)
                        ]
                        for q in range(2)
                    ]
                    reals, imags = [], []
                    for real0, real1, imag0, imag1 in tiles:
                        reals.append(
                            (creal[0] * real0 + cimag[0] * imag0) + (creal[1] * real1 + cimag[1] * imag1)
                        )
                        imags.append(
                            (cimag[0] * real0 - creal[0] * imag0) + (cimag[1] * real1 - creal[1] * imag1)
                        )
                    at = half * CH * 16 + c * 16
                    for q, got in enumerate((reals, imags)):
                        rows = jnp.concatenate(got, axis=0).astype(jnp.bfloat16)
                        cross_ref[q, at : at + 16, lanes] = rows
                        if q == 0:
                            last_sum[at : at + 16] += rows.astype(jnp.float32)

    def add(step, cross_ref):
        chunk = table_ref[pl.ds(step * (SLICE // INNER), SLICE // INNER)].reshape(SLICE, LAGS)
        cos_sum[...] += jnp.dot(cross_ref[0], chunk[:, :HALF], preferred_element_type=jnp.float32)
        sin_sum[...] += jnp.dot(cross_ref[1], chunk[:, HALF:], preferred_element_type=jnp.float32)

    cos_sum[...] = jnp.zeros_like(cos_sum)
    sin_sum[...] = jnp.zeros_like(sin_sum)
    last_sum[...] = jnp.zeros_like(last_sum)
    steps = FREQS // SLICE
    buffers = (even_cross, odd_cross)
    cross(0, even_cross)
    for step in range(1, steps):
        cross(step, buffers[step % 2])
        add(step - 1, buffers[(step - 1) % 2])
    add(steps - 1, buffers[(steps - 1) % 2])

    period = lax.broadcasted_iota(jnp.int32, (8, LANES), 1) + 1
    wave = unit_circle((period * HALF) & (NSAMP - 1))[0].astype(jnp.bfloat16).astype(jnp.float32)
    cos_last = jnp.sum(last_sum[...] * wave[0:1], axis=1, keepdims=True)
    cosines, sines = cos_sum[...], sin_sum[...]
    lane = lax.broadcasted_iota(jnp.int32, (PAIRS, HALF), 1)
    positive = cosines - jnp.where(lane == 0, 0.0, pltpu.roll(sines, 1, 1))
    negative = jnp.where(lane == HALF - 1, cos_last, pltpu.roll(cosines, HALF - 1, 1)) + sines
    first = negative.astype(jnp.bfloat16)
    rest = negative - first.astype(jnp.float32)
    second = rest.astype(jnp.bfloat16)
    third = (rest - second.astype(jnp.float32)).astype(jnp.bfloat16)
    mirror = (
        lax.broadcasted_iota(jnp.int32, (HALF, HALF), 0) + lax.broadcasted_iota(jnp.int32, (HALF, HALF), 1)
        == HALF - 1
    ).astype(jnp.float32).astype(jnp.bfloat16)
    flipped = [jnp.dot(t, mirror, preferred_element_type=jnp.float32) for t in (first, second, third)]
    factor = 1.0 / math.sqrt(FREQS)
    sum_ref[:, :, :, :HALF] = ((flipped[0] + flipped[1] + flipped[2]) * factor).reshape(2, CH, 16, HALF)
    sum_ref[:, :, :, HALF:] = (positive * factor).reshape(2, CH, 16, HALF)

    core = core_ref[0]
    for c in range(CH):
        zero, one = sum_ref[core, c], sum_ref[1 - core, c]
        for x in range(4):
            rows = slice(x * 4, x * 4 + 4)
            out_ref[c, x * 8 : x * 8 + 8, :] = jnp.concatenate([zero[rows], one[rows]], axis=0)


def scattered():
    pairs = []
    for group in range(8):
        for n in range(8):
            pairs.append((group * 8 + n, int(NEAR[group][n]) * 8 + group))
    return pairs


def body(spectra, dead_mask, seg_offsets, src_index):
    pos = {axis: lax.axis_index(axis).astype(jnp.int32) for axis in ("u", "v", "h", "x", "c", "m", "p")}
    wide_pos = (((pos["u"] * 2 + pos["v"]) * 2 + pos["h"]) * 4 + pos["x"]) * 2 + pos["c"]
    far = lax.ppermute(spectra, "m", [(0, 1), (1, 0)])
    width = src_index.shape[0]
    info = jnp.concatenate(
        [
            src_index[None],
            jnp.pad(seg_offsets.T, ((0, 0), (0, width - CH))),
            jnp.pad(dead_mask, (0, width - CH))[None],
            jnp.pad(jnp.stack([wide_pos, pos["m"] * 4 + pos["p"]]), (0, width - 2))[None],
        ]
    )
    pair = jnp.stack([jnp.transpose(t, (2, 1, 0, 3)).reshape(2 * ROWS, SLICE) for t in (spectra, far)])
    pair, info = lax.optimization_barrier((pair, info))
    pieces = lax.all_to_all(jnp.broadcast_to(pair[None], (4,) + pair.shape), "p", 0, 0)

    vmem = pl.BlockSpec(memory_space=pltpu.VMEM)
    smem = pl.BlockSpec(memory_space=pltpu.SMEM)
    chan, src_out = pl.pallas_call(
        whiten_kernel,
        out_shape=(
            jax.ShapeDtypeStruct((FREQS // SLICE, 2, ROWS, SLICE), jnp.float32),
            jax.ShapeDtypeStruct((16, SHARE), jnp.bfloat16),
        ),
        in_specs=[smem, vmem],
        out_specs=(vmem, vmem),
        scratch_shapes=[pltpu.VMEM((2, 2, 16, SHARE), jnp.float32)],
        compiler_params=pltpu.CompilerParams(vmem_limit_bytes=32 * 2**20),
        name="whiten",
    )(info, pieces)

    moved = lax.ppermute(src_out, ("u", "v", "h", "m", "p"), scattered())
    mine = lax.all_to_all(jnp.broadcast_to(moved[None], (8,) + moved.shape), ("v", "x"), 0, 0)
    mine = mine.reshape((2, 4) + moved.shape)
    other = lax.ppermute(mine, "c", [(0, 1), (1, 0)])

    table = pl.pallas_call(
        table_kernel,
        in_specs=[pl.BlockSpec(memory_space=pl.ANY)],
        out_specs=vmem,
        scratch_shapes=[
            pltpu.VMEM((2, INNER, LAGS), jnp.float32),
            pltpu.VMEM((2, LAGS // LANES, FREQS // INNER, LANES), jnp.float32),
        ],
        out_shape=jax.ShapeDtypeStruct((FREQS // INNER, INNER, LAGS), jnp.bfloat16),
        compiler_params=pltpu.CompilerParams(vmem_limit_bytes=16 * 2**20),
        cost_estimate=pl.CostEstimate(flops=4 * FREQS * LAGS, bytes_accessed=2 * FREQS * LAGS, transcendentals=0),
        name="lag_table",
    )(mine)

    out = pl.pallas_call(
        correlate_kernel,
        in_specs=[smem, vmem, vmem, vmem, vmem],
        out_specs=vmem,
        scratch_shapes=[
            pltpu.VMEM((2, PAIRS, SLICE), jnp.bfloat16),
            pltpu.VMEM((2, PAIRS, SLICE), jnp.bfloat16),
            pltpu.VMEM((PAIRS, HALF), jnp.float32),
            pltpu.VMEM((PAIRS, HALF), jnp.float32),
            pltpu.VMEM((PAIRS, LANES), jnp.float32),
            pltpu.VMEM((2, CH, 16, LAGS), jnp.float32),
        ],
        out_shape=jax.ShapeDtypeStruct((CH, 32, LAGS), jnp.float32),
        compiler_params=pltpu.CompilerParams(vmem_limit_bytes=20 * 2**20),
        name="correlate",
    )(pos["c"].reshape(1), mine, other, chan, table)
    return jnp.transpose(out, (1, 0, 2))


def solution(mesh):
    parts = Mesh(mesh.devices.reshape(2, 2, 2, 4, 2, 2, 4), ("u", "v", "h", "x", "c", "m", "p"))
    line = ("m", "p")
    wide = ("u", "v", "h", "x", "c")
    placed = (P(wide, None, None, line), P(wide), P(wide, None), P())
    return jax.shard_map(
        body, mesh=parts, in_specs=placed, out_specs=P(line, wide, None), check_vma=False
    )
```
